256 devices in a mesh: ocean: 32 (over y, z_hi, core), sht: 8 (over z_lo, x).
Axes of the slice: x: 4, y: 4, z: 8 (z_hi: 4, z_lo: 2; z = z_hi * 2 + z_lo), core: 2. Of those that a mesh axis runs over, the one named last changes fastest.
Arguments:
- height: float32 [512, 2048], P('ocean', 'sht'), may hold values from -6 to 6
- east: float32 [512, 2048], P('ocean', 'sht'), may hold values from -3 to 3
- north: float32 [512, 2048], P('ocean', 'sht'), may hold values from -3 to 3
- depth: float32 [512, 2048], P('ocean', 'sht'), may hold values from 0.3 to 1.5
- equilibrium: float32 [512, 2048], P('ocean', 'sht'), may hold values from -3 to 3
- mask: int32 [512, 2048], P('ocean', 'sht'), may hold values from 0 to 1, as said below
- sines: float32 [512], P('ocean'), may hold values from -0.95 to 0.95, as said below
- legendre: float32 [512, 1024, 1024], P('ocean', None, 'sht'), as said below
- love: float32 [1024], replicated, may hold values from 0.01 to 0.3
Outputs:
- level_out: float32 [512, 2048], P('ocean', 'sht')
- east_out: float32 [512, 2048], P('ocean', 'sht')
- north_out: float32 [512, 2048], P('ocean', 'sht')
The draws below stay inside these ranges and needn't reach their ends.
Inputs may be any that keep to these rules, and one draw needn't show every extreme that they name: `mask`: 1 marks ocean, 0 land; rows 0 and 511 and columns 0 and 2047 are land. `sines`: ascending; row j lies within 0.2 / 512 * 1.9 of -0.95 + 1.9 (j + 0.5) / 512. legendre[j, l, m] is the fully normalized associated Legendre function of degree l and order m at sines[j] (unit integral of its square over -1 to 1), zero where l < m.
All inputs are finite; a program needn't handle non-finite values.
Results may differ from the reference program's by a relative error of at most 0.0003.
Values sent between devices are 32-bit elements; how exact they have to be, the bound alone decides.
No kernel may reach another device: no remote copies, remote signals or barrier semaphores. Data moves between devices by JAX's collectives and lax.ppermute only.
A program may use at most 128 MiB of HBM per device.

```python
import math
import jax
import jax.numpy as jnp
from jax import lax

NLON = 2048
LDEG = 1024
MORD = 1024
STEPS = 3
NLAT = 512


def row_sines(key):
    jitter = jax.random.uniform(jax.random.fold_in(key, 5), (NLAT,), jnp.float32, -0.2, 0.2)
    placed = (jnp.arange(NLAT, dtype=jnp.float32) + 0.5 + jitter) / NLAT
    return -0.95 + 1.9 * placed


def draw_sines(key, part):
    return row_sines(key)


def draw_legendre(key, part):
    sines = row_sines(key)
    cosine = jnp.sqrt(1.0 - sines * sines)
    order_int = jnp.arange(MORD, dtype=jnp.int32)
    order = order_int.astype(jnp.float32)
    log_steps = jnp.where(order_int > 0, 0.5 * jnp.log((2.0 * order + 1.0) / jnp.maximum(2.0 * order, 1.0)), 0.0)
    log_diag = jnp.log(jnp.sqrt(0.5)) + jnp.cumsum(log_steps)[None, :] + order[None, :] * jnp.log(cosine)[:, None]
    diagonal = jnp.exp(log_diag)
    second = jnp.sqrt(2.0 * order + 3.0)[None, :] * sines[:, None] * diagonal

    def advance(running, degree):
        latest, before = running
        value_l = degree.astype(jnp.float32)
        factor = jnp.sqrt(jnp.maximum(4.0 * value_l * value_l - 1.0, 1.0) / jnp.maximum(value_l * value_l - order * order, 1.0))
        lower = value_l - 1.0
        prior = jnp.sqrt(jnp.maximum(4.0 * lower * lower - 1.0, 1.0) / jnp.maximum(lower * lower - order * order, 1.0))
        general = factor[None, :] * (sines[:, None] * latest - before / prior[None, :])
        value = jnp.where(degree == order_int[None, :], diagonal, jnp.where(degree == order_int[None, :] + 1, second, jnp.where(degree > order_int[None, :] + 1, general, 0.0)))
        return ((value, latest), value)
    zeros = jnp.zeros((NLAT, MORD), jnp.float32)
    _, stacked = lax.scan(advance, (zeros, zeros), jnp.arange(LDEG, dtype=jnp.int32))
    return jnp.transpose(stacked, (1, 0, 2))


def draw_mask(key, part):
    key = jax.random.fold_in(key, 11)
    cells = jax.random.randint(key, (NLAT, NLON), 0, 4)
    row_index = jnp.arange(NLAT, dtype=jnp.int32)[:, None]
    col_index = jnp.arange(NLON, dtype=jnp.int32)[None, :]
    border = (row_index == 0) | (row_index == NLAT - 1) | (col_index == 0) | (col_index == NLON - 1)
    return jnp.where(border | (cells == 0), 0, 1).astype(jnp.int32)


def level_of(rng, dims, pieces, least, top_value):
    def one(dim, parts):
        heights = jax.random.uniform(jax.random.fold_in(jax.random.fold_in(rng, 6), dim), (parts,), jnp.float32, least / len(pieces), top_value / len(pieces))
        return jnp.repeat(jnp.exp(heights), dims[dim] // parts).reshape((-1,) + (1,) * (len(dims) - dim - 1))

    level = one(*pieces[0])
    for cut in pieces[1:]:
        level = level * one(*cut)
    return level


def gaussian(key, dims, deviation, bound, pieces=(), kind=jnp.bfloat16):
    drawn = deviation * jax.random.normal(key, dims, jnp.float32)
    if pieces:
        drawn = drawn * level_of(key, dims, pieces, -0.22, 0.18)
    return jnp.clip(drawn, -bound, bound).astype(kind)


def setup_inputs(seed: int = 0) -> dict:
    streams_of = jax.random.split(jax.random.key(seed), 10)
    return {
        "height": gaussian(streams_of[0], (NLAT, NLON), 1.0, 6.0, ((0, 32), (1, 8)), jnp.float32),
        "east": gaussian(streams_of[1], (NLAT, NLON), 0.5, 3.0, ((0, 32), (1, 8)), jnp.float32),
        "north": gaussian(streams_of[2], (NLAT, NLON), 0.5, 3.0, ((0, 32), (1, 8)), jnp.float32),
        "depth": jnp.clip(0.3 + 1.2 * jax.random.uniform(streams_of[3], (NLAT, NLON), jnp.float32) ** level_of(streams_of[3], (NLAT, NLON), ((0, 32), (1, 8)), -0.2, 0.2), 0.3, 1.5),
        "equilibrium": gaussian(streams_of[4], (NLAT, NLON), 0.5, 3.0, ((0, 32), (1, 8)), jnp.float32),
        "mask": draw_mask(jax.random.fold_in(streams_of[9], 71), 0),
        "sines": draw_sines(jax.random.fold_in(streams_of[9], 71), 0),
        "legendre": draw_legendre(jax.random.fold_in(streams_of[9], 71), 0),
        "love": jnp.clip(jnp.exp(jax.random.uniform(streams_of[8], (LDEG,), jnp.float32, math.log(0.01), math.log(0.3))), 0.01, 0.3),
    }


COURANT = 0.12
ROTATION = 0.5
FRICTION = 0.3
HIGHEST = lax.Precision.HIGHEST

def self_attraction(level, legendre, love):
    lat_total, lon_total = level.shape
    order_total = legendre.shape[2]
    longitude = jnp.arange(lon_total, dtype=jnp.int32)
    order = jnp.arange(order_total, dtype=jnp.int32)
    phase_index = longitude[:, None] * order[None, :] % lon_total
    angles = phase_index.astype(jnp.float32) * (2.0 * math.pi / lon_total)
    analysis = jnp.concatenate([jnp.cos(angles) / lon_total, -jnp.sin(angles) / lon_total], 1)
    spectra = jnp.dot(level, analysis, precision=HIGHEST, preferred_element_type=jnp.float32)
    weighted = spectra.reshape(lat_total, 2, order_total) * (2.0 / lat_total)
    block_width = min(128, order_total)
    block_count = order_total // block_width

    def one_block(block_index):
        table_block = lax.dynamic_slice_in_dim(legendre, block_index * block_width, block_width, 2)
        spectra_block = lax.dynamic_slice_in_dim(weighted, block_index * block_width, block_width, 2)
        coefs = jnp.einsum('jlm,jcm->lcm', table_block, spectra_block, precision=HIGHEST)
        loaded = coefs * love[:, None, None]
        return jnp.einsum('jlm,lcm->jcm', table_block, loaded, precision=HIGHEST)
    blocks = lax.map(one_block, jnp.arange(block_count, dtype=jnp.int32))
    synth = jnp.transpose(blocks, (1, 2, 0, 3)).reshape(lat_total, 2 * order_total)
    doubling = jnp.where(order == 0, 1.0, 2.0).astype(jnp.float32)[:, None]
    turned = jnp.transpose(angles)
    synthesis = jnp.concatenate([jnp.cos(turned) * doubling, -jnp.sin(turned) * doubling], 0)
    return jnp.dot(synth, synthesis, precision=HIGHEST, preferred_element_type=jnp.float32)

def reference(height, east, north, depth, equilibrium, mask, sines, legendre, love):
    wet_cells = mask == 1
    east_coef = (COURANT / jnp.sqrt(1.0 - sines * sines))[:, None]
    coriolis = (ROTATION * sines)[:, None]
    level = jnp.where(wet_cells, height, 0.0)
    eastward, northward = (east, north)
    damping = FRICTION / depth
    for step_index in range(STEPS):
        sal = self_attraction(level, legendre, love)
        potential = level - sal - equilibrium
        padded = jnp.pad(potential, 1)
        grad_east = east_coef * (padded[1:-1, 2:] - padded[1:-1, :-2])
        grad_north = COURANT * (padded[2:, 1:-1] - padded[:-2, 1:-1])
        new_east = jnp.where(wet_cells, eastward + coriolis * northward - grad_east - damping * eastward, 0.0)
        new_north = jnp.where(wet_cells, northward - coriolis * eastward - grad_north - damping * northward, 0.0)
        flux_east = jnp.pad(depth * new_east, 1)
        flux_north = jnp.pad(depth * new_north, 1)
        divergence = east_coef * (flux_east[1:-1, 2:] - flux_east[1:-1, :-2]) + COURANT * (flux_north[2:, 1:-1] - flux_north[:-2, 1:-1])
        level = jnp.where(wet_cells, level - divergence, 0.0)
        eastward, northward = (new_east, new_north)
    return (level, eastward, northward)
```

```python
import functools

import jax
import jax.numpy as jnp
import ml_dtypes
import numpy as np
from jax import lax
from jax.experimental import pallas as pl
from jax.experimental.pallas import tpu as pltpu
from jax.sharding import PartitionSpec as P

STEPS = 3
COURANT = 0.12
ROTATION = 0.5
FRICTION = 0.3

NLON = 2048
ROWS = 16
COLS = 256
ORD = 128
SHT = 8
OCEAN = 32
CHIPS = OCEAN // 2
LDEG = 1024
HALF = LDEG // 2
CHUNK = HALF // CHIPS
BLOCK = 128
EXT = 384
LANE = 128
EROWS = 32

F32 = jnp.float32
BF16 = jnp.bfloat16


def split(table):
    high = table.astype(ml_dtypes.bfloat16)
    low = (table - high.astype(np.float64)).astype(ml_dtypes.bfloat16)
    return high, low


def tables():
    kappa = np.arange(COLS)[:, None]
    order = np.arange(ORD)[None, :]
    turn = 2.0 * np.pi * (kappa * order % NLON) / NLON
    cosine, sine = np.cos(turn), np.sin(turn)
    analysis = split(np.block([[cosine, -sine], [sine, cosine]]))

    column = np.arange(EXT)
    column = np.where(column < COLS + LANE // 2, column, column - EXT)
    turn = 2.0 * np.pi * (order.T * column[None, :] % NLON) / NLON
    cosine, sine = np.cos(turn), np.sin(turn)
    synthesis = split(np.block([[cosine, sine], [-sine, cosine]]))

    owner = np.arange(SHT)[:, None]
    turn = 2.0 * np.pi * (np.arange(COLS)[None, :] * owner % 16) / 16
    by_owner = np.stack([np.cos(turn), -np.sin(turn)], 1).astype(np.float32)
    turn = 2.0 * np.pi * (np.arange(ORD)[None, :] * owner % 8) / 8
    by_block = np.stack([np.cos(turn), np.sin(turn)], 0).astype(np.float32)
    turn = 2.0 * np.pi * (column[None, :] * owner % 16) / 16
    at_columns = np.stack([np.cos(turn), np.sin(turn)], 0).astype(np.float32)
    doubling = np.full((SHT, 1, ORD), 2.0, np.float32)
    doubling[0, 0, 0] = 1.0
    return analysis, synthesis, by_owner, by_block, at_columns, doubling


def dot3(a, high, low):
    a_high = a.astype(BF16)
    a_low = (a - a_high.astype(F32)).astype(BF16)
    dot = functools.partial(jnp.dot, preferred_element_type=F32)
    return dot(a_high, high) + (dot(a_low, high) + dot(a_high, low))


def start_kernel(height, mask, level, spread):
    value = jnp.where(mask[...] == 1, height[...], 0.0)
    level[...] = value
    for t in range(SHT):
        spread[t] = value


def multiply_rows(weights, legendre, partial):
    wide = [
        [jnp.broadcast_to(weights[c, j : j + 1, :], (8, ORD)) for j in range(ROWS)]
        for c in range(2)
    ]
    for tile in range(BLOCK // 8):
        h, r = divmod(8 * tile, CHUNK)
        sums = [None, None]
        for j in range(ROWS):
            p = legendre[j, 8 * tile : 8 * tile + 8, :]
            for c in range(2):
                term = p * wide[c][j]
                sums[c] = term if sums[c] is None else sums[c] + term
        for c in range(2):
            partial[h, c, r : r + 8, :] = sums[c]


def transform_kernel(half, gathered, rotation, high, low, by_block, legendre, partial, spectra):
    @pl.when(pl.program_id(0) == 0)
    def _():
        z = gathered[...].reshape(SHT * ROWS, COLS)
        a = jnp.concatenate([z * rotation[0:1, :], z * rotation[1:2, :]], 1)
        y = dot3(a, high[...], low[...]).reshape(SHT, ROWS, 2 * ORD)
        re, im = y[:, :, :ORD], y[:, :, ORD:]
        c, s = by_block[0][:, None, :], by_block[1][:, None, :]
        scale = 1.0 / NLON * (2.0 / (ROWS * OCEAN))
        spectra[0] = jnp.sum(re * c + im * s, axis=0) * scale
        spectra[1] = jnp.sum(im * c - re * s, axis=0) * scale

    multiply_rows(spectra[...], legendre, partial)


def rows_kernel(half, spectra, legendre, partial):
    multiply_rows(spectra[...], legendre, partial)


def add_degrees(coefs, legendre, sums):
    acc = [[sums[c, j] for j in range(ROWS)] for c in range(2)]
    for tile in range(BLOCK // 8):
        h, r = divmod(8 * tile, CHUNK)
        x = [coefs[h, c, r : r + 8, :] for c in range(2)]
        for j in range(ROWS):
            p = legendre[j, 8 * tile : 8 * tile + 8, :]
            for c in range(2):
                acc[c][j] = acc[c][j] + p * x[c]
    for c in range(2):
        for j in range(ROWS):
            sums[c, j] = acc[c][j]


def degrees_kernel(half, coefs, legendre, sums):
    @pl.when(pl.program_id(0) == 0)
    def _():
        sums[...] = jnp.zeros_like(sums)

    add_degrees(coefs, legendre, sums)


def finish_kernel(half, before, coefs, legendre, spread, sums, synth):
    @pl.when(pl.program_id(0) == 0)
    def _():
        sums[...] = before[...]

    add_degrees(coefs, legendre, sums)

    @pl.when(pl.program_id(0) == pl.num_programs(0) - 1)
    def _():
        for c in range(2):
            for j in range(ROWS):
                synth[c, j : j + 1, :] = jnp.sum(sums[c, j], axis=0, keepdims=True)
        value = synth[...]
        for t in range(SHT):
            spread[t] = value


def potential_kernel(
    place, synth, rotation, doubling, high, low, at_columns, gathered, equilibrium, pot, first, last
):
    t = place[0]
    c, s = rotation[0:1, :][None], rotation[1:2, :][None]
    e = doubling[...]
    s0, s1 = synth[:, 0] * e, synth[:, 1] * e
    vr = (s0 * c - s1 * s).reshape(SHT * ROWS, ORD)
    vi = (s0 * s + s1 * c).reshape(SHT * ROWS, ORD)
    g = dot3(jnp.concatenate([vr, vi], 1), high[...], low[...]).reshape(SHT, ROWS, 2 * EXT)
    sal = jnp.sum(
        g[:, :, :EXT] * at_columns[0][:, None, :] - g[:, :, EXT:] * at_columns[1][:, None, :], axis=0
    )
    right = gathered[lax.rem(t + 1, SHT)][:, :LANE]
    left = gathered[lax.rem(t + SHT - 1, SHT)][:, LANE:]
    lane = lax.broadcasted_iota(jnp.int32, (ROWS, LANE), 1)
    level = jnp.concatenate([gathered[t], jnp.where(lane < LANE // 2, right, left)], 1)
    pot[...] = level - sal - equilibrium[...]
    first[...] = pot[0:2, :]
    last[...] = pot[ROWS - 2 : ROWS, :]


def step_kernel(
    place, pot, above, below, east, north, depth, wet, damping, east_coef, coriolis, gathered, *rest
):
    *outs, field = rest
    field[...] = jnp.zeros_like(field)
    field[6:8, :] = above[...]
    field[8:24, :] = pot[...]
    field[24:26, :] = below[...]
    p = field[...]
    plus_col = lambda x: pltpu.roll(x, EXT - 1, 1)
    minus_col = lambda x: pltpu.roll(x, 1, 1)
    plus_row = lambda x: pltpu.roll(x, EROWS - 1, 0)
    minus_row = lambda x: pltpu.roll(x, 1, 0)
    ec = east_coef[...]
    u, v, f, d = east[...], north[...], coriolis[...], damping[...]
    ocean = wet[...] > 0.5
    grad_east = ec * (plus_col(p) - minus_col(p))
    grad_north = COURANT * (plus_row(p) - minus_row(p))
    new_u = jnp.where(ocean, u + f * v - grad_east - d * u, 0.0)
    new_v = jnp.where(ocean, v - f * u - grad_north - d * v, 0.0)
    flux_u, flux_v = depth[...] * new_u, depth[...] * new_v
    div = ec * (plus_col(flux_u) - minus_col(flux_u)) + COURANT * (
        plus_row(flux_v) - minus_row(flux_v)
    )
    inner = (slice(8, 24), slice(0, COLS))
    level = jnp.where(ocean[inner], gathered[place[0]] - div[inner], 0.0)
    if len(outs) == 3 and outs[0].shape == (EROWS, EXT):
        outs[0][...] = new_u
        outs[1][...] = new_v
        for t in range(SHT):
            outs[2][t] = level
    else:
        outs[0][...] = level
        outs[1][...] = new_u[inner]
        outs[2][...] = new_v[inner]


def shape(*dims):
    return jax.ShapeDtypeStruct(dims, F32)


PARAMS = pltpu.CompilerParams(vmem_limit_bytes=56 * 1024 * 1024)
COST = pl.CostEstimate(flops=2 * ROWS * HALF * ORD * 2, bytes_accessed=9 << 20, transcendentals=0)
WHOLE = pl.BlockSpec(memory_space=pltpu.VMEM)
SCALAR = pl.BlockSpec(memory_space=pltpu.SMEM)


def streamed(kernel, in_specs, out_specs, out_shape, scratch=()):
    return pl.pallas_call(
        kernel,
        grid_spec=pltpu.PrefetchScalarGridSpec(
            num_scalar_prefetch=1,
            grid=(HALF // BLOCK,),
            in_specs=in_specs,
            out_specs=out_specs,
            scratch_shapes=list(scratch),
        ),
        out_shape=out_shape,
        compiler_params=PARAMS,
        cost_estimate=COST,
    )


def fixed(*dims):
    return pl.BlockSpec(dims, lambda i, half: (0,) * len(dims))


LEGENDRE = pl.BlockSpec((ROWS, BLOCK, ORD), lambda i, half: (0, half[0] * (HALF // BLOCK) + i, 0))
COEFS = pl.BlockSpec((BLOCK // CHUNK, 2, CHUNK, ORD), lambda i, half: (i, 0, 0, 0))


def per_device(height, east, north, depth, equilibrium, mask, sines, legendre, love):
    analysis, synthesis, by_owner, by_block, at_columns, doubling = tables()
    sht = lax.axis_index("sht")
    ocean = lax.axis_index("ocean")
    core = lax.rem(ocean, 2)
    place = sht.astype(jnp.int32).reshape(1)
    own_half = core.astype(jnp.int32).reshape(1)
    other_half = 1 - own_half
    owner_rotation = lax.dynamic_index_in_dim(jnp.asarray(by_owner), sht, 0, False)
    block_rotation = lax.dynamic_index_in_dim(jnp.asarray(by_block), sht, 1, False)
    a_high, a_low = (jnp.asarray(x) for x in analysis)
    s_high, s_low = (jnp.asarray(x) for x in synthesis)

    cores = [(i, i ^ 1) for i in range(OCEAN)]
    groups = [[2 * h + c for h in range(CHIPS)] for c in range(2)]
    next_row = [(i, i + 1) for i in range(OCEAN - 1)]
    prev_row = [(j, i) for i, j in next_row]
    next_col = [(i, i + 1) for i in range(SHT - 1)]
    prev_col = [(j, i) for i, j in next_col]

    level, spread = pl.pallas_call(
        start_kernel,
        in_specs=[WHOLE, WHOLE],
        out_specs=[WHOLE, WHOLE],
        out_shape=[shape(ROWS, COLS), shape(SHT, ROWS, COLS)],
    )(height, mask)

    wet = (mask == 1).astype(F32)
    stack = jnp.stack([equilibrium, east, north, depth, wet])
    from_right = lax.ppermute(stack[:, :, :LANE], "sht", prev_col)
    from_left = lax.ppermute(stack[:, :, COLS - LANE :], "sht", next_col)
    lane = lax.broadcasted_iota(jnp.int32, from_right.shape, 2)
    stack = jnp.concatenate([stack, jnp.where(lane < LANE // 2, from_right, from_left)], 2)
    equilibrium_ext = stack[0]
    stack = jnp.concatenate(
        [stack[1:], jnp.broadcast_to(sines[None, :, None], (1, ROWS, EXT))], 0
    )
    from_below = lax.ppermute(stack[:, :8], "ocean", prev_row)
    from_above = lax.ppermute(stack[:, ROWS - 8 :], "ocean", next_row)
    stack = jnp.concatenate([from_above, stack, from_below], 1)
    u, v, depth_ext, wet_ext, sines_ext = (stack[i] for i in range(5))
    damping = FRICTION / jnp.where(wet_ext > 0.5, depth_ext, 1.0)
    east_coef = COURANT / jnp.sqrt(1.0 - sines_ext * sines_ext)
    coriolis = ROTATION * sines_ext

    own_chunk = core * HALF + (ocean // 2) * CHUNK
    own_love = lax.dynamic_slice_in_dim(love, own_chunk, CHUNK)[None, :, None]

    partial_shape = shape(CHIPS, 2, CHUNK, ORD)
    for step_index in range(STEPS):
        gathered = lax.all_to_all(spread, "sht", 0, 0, tiled=True)
        given, spectra = streamed(
            transform_kernel,
            [
                fixed(SHT, ROWS, COLS),
                fixed(2, COLS),
                fixed(2 * COLS, 2 * ORD),
                fixed(2 * COLS, 2 * ORD),
                fixed(2, SHT, ORD),
                LEGENDRE,
            ],
            [COEFS, fixed(2, ROWS, ORD)],
            [partial_shape, shape(2, ROWS, ORD)],
        )(other_half, gathered, owner_rotation, a_high, a_low, by_block, legendre)
        taken = lax.ppermute(given, "ocean", cores)
        kept = streamed(rows_kernel, [fixed(2, ROWS, ORD), LEGENDRE], COEFS, partial_shape)(
            own_half, spectra, legendre
        )
        parts = lax.all_to_all(
            kept + taken, "ocean", 0, 0, tiled=True, axis_index_groups=groups
        )
        loaded = jnp.sum(parts, axis=0) * own_love
        own = lax.all_to_all(
            jnp.broadcast_to(loaded[None], (CHIPS, 2, CHUNK, ORD)),
            "ocean",
            0,
            0,
            tiled=True,
            axis_index_groups=groups,
        )
        other = lax.ppermute(own, "ocean", cores)
        sums = streamed(
            degrees_kernel, [COEFS, LEGENDRE], fixed(2, ROWS, 8, ORD), shape(2, ROWS, 8, ORD)
        )(own_half, own, legendre)
        synth_spread = streamed(
            finish_kernel,
            [fixed(2, ROWS, 8, ORD), COEFS, LEGENDRE],
            fixed(SHT, 2, ROWS, ORD),
            shape(SHT, 2, ROWS, ORD),
            [pltpu.VMEM((2, ROWS, 8, ORD), F32), pltpu.VMEM((2, ROWS, ORD), F32)],
        )(other_half, sums, other, legendre)
        synth = lax.all_to_all(synth_spread, "sht", 0, 0, tiled=True)
        pot, first, last = pl.pallas_call(
            potential_kernel,
            in_specs=[SCALAR] + [WHOLE] * 8,
            out_specs=[WHOLE] * 3,
            out_shape=[shape(ROWS, EXT), shape(2, EXT), shape(2, EXT)],
            compiler_params=PARAMS,
        )(
            place,
            synth,
            block_rotation,
            doubling,
            s_high,
            s_low,
            at_columns,
            gathered,
            equilibrium_ext,
        )
        below = lax.ppermute(first, "ocean", prev_row)
        above = lax.ppermute(last, "ocean", next_row)
        final = step_index == STEPS - 1
        block = shape(ROWS, COLS)
        extended = shape(EROWS, EXT)
        results = pl.pallas_call(
            step_kernel,
            in_specs=[SCALAR] + [WHOLE] * 11,
            out_specs=[WHOLE] * 3,
            out_shape=[block] * 3 if final else [extended, extended, shape(SHT, ROWS, COLS)],
            scratch_shapes=[pltpu.VMEM((EROWS, EXT), F32)],
            compiler_params=PARAMS,
        )(
            place,
            pot,
            above,
            below,
            u,
            v,
            depth_ext,
            wet_ext,
            damping,
            east_coef,
            coriolis,
            gathered,
        )
        if final:
            return tuple(results)
        u, v, spread = results


def solution(mesh):
    in_specs = (
        P("ocean", "sht"),
        P("ocean", "sht"),
        P("ocean", "sht"),
        P("ocean", "sht"),
        P("ocean", "sht"),
        P("ocean", "sht"),
        P("ocean"),
        P("ocean", None, "sht"),
        P(),
    )
    out_specs = (P("ocean", "sht"), P("ocean", "sht"), P("ocean", "sht"))
    return jax.shard_map(
        per_device, mesh=mesh, in_specs=in_specs, out_specs=out_specs, check_vma=False
    )
```

```python
import functools

import jax
import jax.numpy as jnp
import ml_dtypes
import numpy as np
from jax import lax
from jax.experimental import pallas as pl
from jax.experimental.pallas import tpu as pltpu
from jax.sharding import PartitionSpec as P

STEPS = 3
COURANT = 0.12
ROTATION = 0.5
FRICTION = 0.3

NLON = 2048
ROWS = 16
COLS = 256
ORD = 128
SHT = 8
OCEAN = 32
LDEG = 1024
CHUNK = 128
PEERS = 4
EROWS = 32
FIELDS = 5

F32 = jnp.float32
BF16 = jnp.bfloat16


def split(table):
    high = table.astype(ml_dtypes.bfloat16)
    low = (table - high.astype(np.float64)).astype(ml_dtypes.bfloat16)
    return high, low


def tables():
    kappa = np.arange(COLS)[:, None]
    order = np.arange(ORD)[None, :]
    turn = 2.0 * np.pi * (kappa * order % NLON) / NLON
    cosine, sine = np.cos(turn), np.sin(turn)
    analysis = np.stack(split(np.block([[cosine, sine]])))
    cosine, sine = cosine.T, sine.T
    synthesis = split(np.block([[cosine, sine], [-sine, cosine]]))

    owner = np.arange(SHT)[:, None]
    turn = 2.0 * np.pi * (np.arange(COLS)[None, :] * owner % 16) / 16
    by_owner = np.stack([np.cos(turn), np.sin(turn)], 0).astype(np.float32)
    turn = 2.0 * np.pi * (np.arange(ORD)[None, :] * owner % 8) / 8
    by_block = np.stack([np.cos(turn), np.sin(turn)], 0).astype(np.float32)
    doubling = np.full((SHT, 1, ORD), 2.0, np.float32)
    doubling[0, 0, 0] = 1.0
    turns = np.concatenate([by_owner, by_block], 2)
    return analysis, synthesis, turns, doubling


def dot3(a, high, low):
    a_high = a.astype(BF16)
    a_low = (a - a_high.astype(F32)).astype(BF16)
    dot = functools.partial(jnp.dot, preferred_element_type=F32)
    return dot(a_high, high) + (dot(a_low, high) + dot(a_high, low))


def start_kernel(height, equilibrium, east, north, depth, mask, spread, floats, ints, sems):
    copies = [
        pltpu.make_async_copy(source, floats.at[i], sems.at[i])
        for i, source in enumerate((height, equilibrium, east, north, depth))
    ]
    copies.append(pltpu.make_async_copy(mask, ints, sems.at[5]))
    for copy in copies:
        copy.start()
    for copy in copies:
        copy.wait()
    ocean = ints[...] == 1
    for i in range(FIELDS):
        field = floats[i]
        if i in (0, FIELDS - 1):
            field = jnp.where(ocean, field, 0.0)
        for t in range(SHT):
            spread[t, ROWS * i : ROWS * (i + 1), :] = field


def degrees_of(half, y, k, tile):
    first = (half * PEERS + (y ^ k)) * CHUNK + tile * 8
    return pl.ds(pl.multiple_of(first, 8), 8)


def multiply_rows(half, y, weights, legendre, partial):
    wide = [
        [jnp.broadcast_to(weights[c, j : j + 1, :], (8, ORD)) for j in range(ROWS)]
        for c in range(2)
    ]

    def some(i, _):
        for k in range(PEERS):
            for n in range(2):
                tile = 2 * i + n
                degrees = degrees_of(half, y, k, tile)
                sums = [None, None]
                for j in range(ROWS):
                    p = legendre[j, degrees, :]
                    for c in range(2):
                        term = p * wide[c][j]
                        sums[c] = term if sums[c] is None else sums[c] + term
                for c in range(2):
                    partial[k, c, pl.ds(pl.multiple_of(8 * tile, 8), 8), :] = sums[c]
        return 0

    lax.fori_loop(0, CHUNK // 16, some, 0)


def transform_kernel(sht, core, y, level, turns, table, legendre, partial, spectra):
    z = level[:, 0:ROWS, :].reshape(SHT * ROWS, COLS)
    c, s = turns[0, pl.ds(sht[0], 1), :COLS], turns[1, pl.ds(sht[0], 1), :COLS]
    a = jnp.concatenate([z * c, z * -s], 0)
    out = dot3(a, table[0], table[1]).reshape(2, SHT, ROWS, 2 * ORD)
    re = out[0, :, :, :ORD] + out[1, :, :, ORD:]
    im = out[1, :, :, :ORD] - out[0, :, :, ORD:]
    c, s = turns[0, :, COLS:][:, None, :], turns[1, :, COLS:][:, None, :]
    scale = 1.0 / NLON * (2.0 / (ROWS * OCEAN))
    spectra[0] = jnp.sum(re * c + im * s, axis=0) * scale
    spectra[1] = jnp.sum(im * c - re * s, axis=0) * scale
    multiply_rows(1 - core[0], y[0], spectra[...], legendre, partial)


def rows_kernel(core, y, spectra, legendre, partial):
    multiply_rows(core[0], y[0], spectra[...], legendre, partial)


def column_of(line):
    n = line.shape[1]
    row = lax.broadcasted_iota(jnp.int32, (n, n), 0)
    lane = lax.broadcasted_iota(jnp.int32, (n, n), 1)
    return jnp.sum(jnp.where(row == lane, line, 0.0), axis=1, keepdims=True)


def love_kernel(core, y, own, one, two, three, love, loaded):
    factor = column_of(love[pl.ds(core[0] * PEERS + y[0], 1), :])
    for c in range(2):
        loaded[c] = ((own[c] + one[c]) + (two[c] + three[c])) * factor


def add_degrees(half, y, before, coefs, legendre):
    def some(i, acc):
        acc = list(acc)
        for k in range(PEERS):
            for n in range(2):
                tile = 2 * i + n
                degrees = degrees_of(half, y, k, tile)
                at = pl.ds(pl.multiple_of(8 * tile, 8), 8)
                x = [coefs[k][c, at, :] for c in range(2)]
                for j in range(ROWS):
                    p = legendre[j, degrees, :]
                    for c in range(2):
                        acc[c * ROWS + j] = acc[c * ROWS + j] + p * x[c]
        return tuple(acc)

    return lax.fori_loop(0, CHUNK // 16, some, tuple(before))


def degrees_kernel(core, y, *refs):
    *coefs, legendre, sums = refs
    zero = jnp.zeros((8, ORD), F32)
    acc = add_degrees(core[0], y[0], [zero] * (2 * ROWS), coefs, legendre)
    for i in range(2 * ROWS):
        sums[i] = acc[i]


def finish_kernel(core, y, before, *refs):
    *coefs, legendre, spread, synth = refs
    acc = add_degrees(1 - core[0], y[0], [before[i] for i in range(2 * ROWS)], coefs, legendre)
    for i in range(2 * ROWS):
        synth[i : i + 1, :] = jnp.sum(acc[i], axis=0, keepdims=True)
    value = synth[...]
    for t in range(SHT):
        spread[t] = value


def potential_kernel(
    core, synth, turns, doubling, high, low, level, fields, *rest
):
    *sines, pot, to_core, to_chip, sides, edges = rest
    e = doubling[...]
    s0, s1 = synth[:, 0:ROWS, :] * e, synth[:, ROWS:, :] * e
    for t in range(SHT):
        rows = slice(SHT * ROWS * t, SHT * ROWS * (t + 1))
        c, s = turns[0, t : t + 1, COLS:][None], turns[1, t : t + 1, COLS:][None]
        sides[rows, :ORD] = (s0 * c - s1 * s).reshape(SHT * ROWS, ORD)
        sides[rows, ORD:] = (s0 * s + s1 * c).reshape(SHT * ROWS, ORD)
    g = dot3(sides[...], high[...], low[...]).reshape(SHT, SHT, ROWS, 2 * COLS)
    c, s = turns[0, :, :COLS][:, None, :], turns[1, :, :COLS][:, None, :]
    for t in range(SHT):
        sal = jnp.sum(g[t, :, :, :COLS] * c - g[t, :, :, COLS:] * s, axis=0)
        value = level[t, 0:ROWS, :] - sal - fields[t, ROWS : 2 * ROWS, :]
        cols = slice(COLS * t, COLS * (t + 1))
        pot[:, cols] = value
        edges[0, 0:2, cols] = value[0:2, :]
        edges[1, 0:2, cols] = value[ROWS - 2 :, :]
        if sines:
            for side, row in ((0, 0), (1, ROWS - 1)):
                for i in range(3):
                    at = ROWS * (i + 2) + row
                    edges[side, 2 + i : 3 + i, cols] = fields[t, at : at + 1, :]
    if sines:
        wide = column_of(sines[0][...])
        for side, row in ((0, 0), (1, ROWS - 1)):
            edges[side, 5:6, :] = jnp.broadcast_to(wide[row : row + 1, :], (1, NLON))
            edges[side, 6:8, :] = jnp.zeros((2, NLON), F32)
    first_core = core[0] == 0
    to_core[...] = jnp.where(first_core, edges[1], edges[0])
    to_chip[...] = jnp.where(first_core, edges[0], edges[1])


def above_and_below(core, from_core, from_chip):
    first_core = core[0] == 0
    a, b = from_core[...], from_chip[...]
    return jnp.where(first_core, b, a), jnp.where(first_core, a, b)


def advance(field, pot, above, below, u, v, depth, damping, east_coef, coriolis):
    field[0:8, :] = jnp.zeros((8, NLON), F32)
    field[24:32, :] = jnp.zeros((8, NLON), F32)
    field[6:8, :] = above
    field[8:24, :] = pot[...]
    field[24:26, :] = below
    p = field[...]
    plus_col = lambda x: pltpu.roll(x, NLON - 1, 1)
    minus_col = lambda x: pltpu.roll(x, 1, 1)
    plus_row = lambda x: pltpu.roll(x, EROWS - 1, 0)
    minus_row = lambda x: pltpu.roll(x, 1, 0)
    ec = east_coef[...]
    old_u, old_v, f, d = u[...], v[...], coriolis[...], damping[...]
    ocean = depth[...] > 0.0
    grad_east = ec * (plus_col(p) - minus_col(p))
    grad_north = COURANT * (plus_row(p) - minus_row(p))
    new_u = jnp.where(ocean, old_u + f * old_v - grad_east - d * old_u, 0.0)
    new_v = jnp.where(ocean, old_v - f * old_u - grad_north - d * old_v, 0.0)
    flux_u, flux_v = depth[...] * new_u, depth[...] * new_v
    div = ec * (plus_col(flux_u) - minus_col(flux_u)) + COURANT * (
        plus_row(flux_v) - minus_row(flux_v)
    )
    return new_u, new_v, div, ocean


INNER = slice(8, 24)


def store_level(out, level, div, ocean):
    for t in range(SHT):
        cols = slice(COLS * t, COLS * (t + 1))
        out[t] = jnp.where(ocean[INNER, cols], level[t, 0:ROWS, :] - div[INNER, cols], 0.0)


def first_step_kernel(
    core, pot, from_core, from_chip, fields, sines,
    u, v, level, depth, damping, east_coef, coriolis, field,
):
    above, below = above_and_below(core, from_core, from_chip)
    for i, out in enumerate((u, v, depth)):
        for halo in (0, EROWS - 8):
            out[halo : halo + 8, :] = jnp.zeros((8, NLON), F32)
        out[7:8, :] = above[2 + i : 3 + i, :]
        out[24:25, :] = below[2 + i : 3 + i, :]
        for t in range(SHT):
            at = ROWS * (i + 2)
            out[INNER, COLS * t : COLS * (t + 1)] = fields[t, at : at + ROWS, :]
    coriolis[...] = jnp.zeros_like(coriolis)
    coriolis[7:8, :] = above[5:6, :]
    coriolis[INNER, :] = jnp.broadcast_to(column_of(sines[...]), (ROWS, NLON))
    coriolis[24:25, :] = below[5:6, :]
    x = coriolis[...]
    coriolis[...] = ROTATION * x
    east_coef[...] = COURANT / jnp.sqrt(1.0 - x * x)
    damping[...] = FRICTION / jnp.where(depth[...] > 0.0, depth[...], 1.0)
    new_u, new_v, div, ocean = advance(
        field, pot, above[0:2], below[0:2], u, v, depth, damping, east_coef, coriolis
    )
    u[...] = new_u
    v[...] = new_v
    store_level(level, fields, div, ocean)


def step_kernel(
    core, pot, from_core, from_chip, old_level, old_u, old_v, depth, damping, east_coef, coriolis,
    u, v, level, field,
):
    above, below = above_and_below(core, from_core, from_chip)
    new_u, new_v, div, ocean = advance(
        field, pot, above, below, old_u, old_v, depth, damping, east_coef, coriolis
    )
    u[...] = new_u
    v[...] = new_v
    store_level(level, old_level, div, ocean)


def last_step_kernel(
    sht, core, pot, from_core, from_chip, old_level, old_u, old_v, depth, damping, east_coef, coriolis,
    level, u, v, field,
):
    above, below = above_and_below(core, from_core, from_chip)
    new_u, new_v, div, _ = advance(
        field, pot, above, below, old_u, old_v, depth, damping, east_coef, coriolis
    )
    own = pl.ds(pl.multiple_of(sht[0] * COLS, COLS), COLS)
    field[...] = new_u
    u[...] = field[INNER, own]
    field[...] = new_v
    v[...] = field[INNER, own]
    field[...] = div
    level[...] = jnp.where(depth[INNER, own] > 0.0, old_level[sht[0]] - field[INNER, own], 0.0)


def shape(*dims):
    return jax.ShapeDtypeStruct(dims, F32)


PARAMS = pltpu.CompilerParams(vmem_limit_bytes=16 * 1024 * 1024)
START_PARAMS = pltpu.CompilerParams(vmem_limit_bytes=60 * 1024 * 1024)
COST = pl.CostEstimate(flops=ROWS * LDEG * ORD * 2, bytes_accessed=5 << 20, transcendentals=0)
WHOLE = pl.BlockSpec(memory_space=pltpu.VMEM)
SCALAR = pl.BlockSpec(memory_space=pltpu.SMEM)
HBM = pl.BlockSpec(memory_space=pltpu.HBM)


def whole(kernel, out_shape, scalars, *args, scratch=(), cost=None):
    return pl.pallas_call(
        kernel,
        in_specs=[SCALAR] * len(scalars) + [WHOLE] * len(args),
        out_specs=[WHOLE] * len(out_shape),
        out_shape=out_shape,
        scratch_shapes=list(scratch),
        compiler_params=PARAMS,
        cost_estimate=cost,
    )(*scalars, *args)


def per_device(height, east, north, depth, equilibrium, mask, sines, legendre, love):
    analysis, (s_high, s_low), turns, doubling = tables()
    ocean = lax.axis_index("ocean").astype(jnp.int32)
    sht = lax.axis_index("sht").astype(jnp.int32).reshape(1)
    core = (ocean & 1).reshape(1)
    y = (ocean >> 3).reshape(1)
    sines = sines.reshape(1, ROWS)
    love = love.reshape(LDEG // CHUNK, CHUNK)

    def swap(x, k):
        return lax.ppermute(x, "ocean", [(i, i ^ k) for i in range(OCEAN)])

    def swap_ring(x, k):
        pairs = [
            (SHT * i + t, SHT * (i ^ k) + t)
            for i in range(OCEAN)
            for t in range(SHT)
            if CHUNK * ((i % 2) * PEERS + i // 8 + 1) > ORD * t
        ]
        return lax.ppermute(x, ("ocean", "sht"), pairs)

    along_y = (8, 16, 24)
    along_z = (2, 4, 6)
    chips = [(i, i + 1 if i % 2 else i - 1) for i in range(1, OCEAN - 1)]

    spread = pl.pallas_call(
        start_kernel,
        in_specs=[HBM] * 6,
        out_specs=WHOLE,
        out_shape=shape(SHT, FIELDS * ROWS, COLS),
        scratch_shapes=[
            pltpu.VMEM((FIELDS, ROWS, COLS), F32),
            pltpu.VMEM((ROWS, COLS), jnp.int32),
            pltpu.SemaphoreType.DMA((6,)),
        ],
        compiler_params=START_PARAMS,
    )(height, equilibrium, east, north, depth, mask)
    spread, sht, core, y = lax.optimization_barrier((spread, sht, core, y))
    fields = lax.all_to_all(spread, "sht", 0, 0, tiled=True)

    extended = shape(EROWS, NLON)
    block = shape(ROWS, COLS)
    partial = shape(PEERS, 2, CHUNK, ORD)
    field = [pltpu.VMEM((EROWS, NLON), F32)]
    level = fields
    for step in range(STEPS):
        given, spectra = whole(
            transform_kernel,
            [partial, shape(2, ROWS, ORD)],
            (sht, core, y),
            *(level, turns, analysis, legendre),
            cost=COST,
        )
        taken = swap(given, 1)
        (kept,) = whole(rows_kernel, [partial], (core, y), spectra, legendre, cost=COST)
        parts = [kept[k] + taken[k] for k in range(PEERS)]
        others = [swap(parts[k], along_y[k - 1]) for k in range(1, PEERS)]
        ring = (parts[0] + others[0]) + (others[1] + others[2])
        rings = [swap_ring(ring, k) for k in along_z]
        (coefs,) = whole(
            love_kernel, [shape(2, CHUNK, ORD)], (core, y), ring, *rings, love
        )
        own_coefs = [coefs] + [swap(coefs, k) for k in along_y]
        other_coefs = [swap(x, 1) for x in own_coefs]
        (sums,) = whole(
            degrees_kernel,
            [shape(2 * ROWS, 8, ORD)],
            (core, y),
            *(*own_coefs, legendre),
            cost=COST,
        )
        (synth_spread,) = whole(
            finish_kernel,
            [shape(SHT, 2 * ROWS, ORD)],
            (core, y),
            *(sums, *other_coefs, legendre),
            scratch=[pltpu.VMEM((2 * ROWS, ORD), F32)],
            cost=COST,
        )
        synth = lax.all_to_all(synth_spread, "sht", 0, 0, tiled=True)
        halo = 8 if step == 0 else 2
        pot, to_core, to_chip = whole(
            potential_kernel,
            [shape(ROWS, NLON), shape(halo, NLON), shape(halo, NLON)],
            (core,),
            *(synth, turns, doubling, s_high, s_low, level, fields),
            *([sines] if step == 0 else []),
            scratch=[
                pltpu.VMEM((SHT * SHT * ROWS, 2 * ORD), F32),
                pltpu.VMEM((2, halo, NLON), F32),
            ],
        )
        from_chip = lax.ppermute(to_chip, "ocean", chips)
        from_core = swap(to_core, 1)
        given = (pot, from_core, from_chip)
        if step == 0:
            u, v, level, *constants = whole(
                first_step_kernel,
                [extended, extended, shape(SHT, ROWS, COLS)] + [extended] * 4,
                (core,),
                *(*given, fields, sines),
                scratch=field,
            )
        elif step < STEPS - 1:
            u, v, level = whole(
                step_kernel,
                [extended, extended, shape(SHT, ROWS, COLS)],
                (core,),
                *(*given, level, u, v, *constants),
                scratch=field,
            )
        else:
            level, u, v = whole(
                last_step_kernel,
                [block] * 3,
                (sht, core),
                *(*given, level, u, v, *constants),
                scratch=field,
            )
    return level, u, v


def solution(mesh):
    in_specs = (
        P("ocean", "sht"),
        P("ocean", "sht"),
        P("ocean", "sht"),
        P("ocean", "sht"),
        P("ocean", "sht"),
        P("ocean", "sht"),
        P("ocean"),
        P("ocean", None, "sht"),
        P(),
    )
    out_specs = (P("ocean", "sht"), P("ocean", "sht"), P("ocean", "sht"))
    return jax.shard_map(
        per_device, mesh=mesh, in_specs=in_specs, out_specs=out_specs, check_vma=False
    )
```

```python
import functools

import jax
import jax.numpy as jnp
import ml_dtypes
import numpy as np
from jax import lax
from jax.experimental import pallas as pl
from jax.experimental.pallas import tpu as pltpu
from jax.sharding import PartitionSpec as P

STEPS = 3
COURANT = 0.12
ROTATION = 0.5
FRICTION = 0.3

NLON = 2048
ROWS = 16
COLS = 256
ORD = 128
SHT = 8
OCEAN = 32
LDEG = 1024
CHUNK = 128
PEERS = 4
EROWS = 32
FIELDS = 5

F32 = jnp.float32
BF16 = jnp.bfloat16


def split(table):
    high = table.astype(ml_dtypes.bfloat16)
    low = (table - high.astype(np.float64)).astype(ml_dtypes.bfloat16)
    return high, low


def tables():
    kappa = np.arange(COLS)[:, None]
    order = np.arange(ORD)[None, :]
    turn = 2.0 * np.pi * (kappa * order % NLON) / NLON
    cosine, sine = np.cos(turn), np.sin(turn)
    analysis = np.stack(split(np.block([[cosine, sine]])))
    cosine, sine = cosine.T, sine.T
    synthesis = split(np.block([[cosine, sine], [-sine, cosine]]))

    owner = np.arange(SHT)[:, None]
    turn = 2.0 * np.pi * (np.arange(COLS)[None, :] * owner % 16) / 16
    by_owner = np.stack([np.cos(turn), np.sin(turn)], 0).astype(np.float32)
    turn = 2.0 * np.pi * (np.arange(ORD)[None, :] * owner % 8) / 8
    by_block = np.stack([np.cos(turn), np.sin(turn)], 0).astype(np.float32)
    doubling = np.full((SHT, 1, ORD), 2.0, np.float32)
    doubling[0, 0, 0] = 1.0
    turns = np.concatenate([by_owner, by_block], 2)
    return analysis, synthesis, turns, doubling


def dot3(a, high, low):
    a_high = a.astype(BF16)
    a_low = (a - a_high.astype(F32)).astype(BF16)
    dot = functools.partial(jnp.dot, preferred_element_type=F32)
    return dot(a_high, high) + (dot(a_low, high) + dot(a_high, low))


def start_kernel(height, equilibrium, east, north, depth, mask, spread, floats, ints, sems):
    copies = [
        pltpu.make_async_copy(source, floats.at[i], sems.at[i])
        for i, source in enumerate((height, equilibrium, east, north, depth))
    ]
    copies.append(pltpu.make_async_copy(mask, ints, sems.at[5]))
    for copy in copies:
        copy.start()
    for copy in copies:
        copy.wait()
    ocean = ints[...] == 1
    for i in range(FIELDS):
        field = floats[i]
        if i in (0, FIELDS - 1):
            field = jnp.where(ocean, field, 0.0)
        for t in range(SHT):
            spread[t, ROWS * i : ROWS * (i + 1), :] = field


def degrees_of(half, y, k, tile):
    first = (half * PEERS + (y ^ k)) * CHUNK + tile * 8
    return pl.ds(pl.multiple_of(first, 8), 8)


def multiply_rows(half, y, weights, legendre, partial):
    wide = [
        [jnp.broadcast_to(weights[c, j : j + 1, :], (8, ORD)) for j in range(ROWS)]
        for c in range(2)
    ]

    def some(i, _):
        for k in range(PEERS):
            for n in range(2):
                tile = 2 * i + n
                degrees = degrees_of(half, y, k, tile)
                sums = [None, None]
                for j in range(ROWS):
                    p = legendre[j, degrees, :]
                    for c in range(2):
                        term = p * wide[c][j]
                        sums[c] = term if sums[c] is None else sums[c] + term
                for c in range(2):
                    partial[k, c, pl.ds(pl.multiple_of(8 * tile, 8), 8), :] = sums[c]
        return 0

    lax.fori_loop(0, CHUNK // 16, some, 0)


def transform_kernel(sht, core, y, level, turns, table, legendre, partial, spectra):
    z = level[:, 0:ROWS, :].reshape(SHT * ROWS, COLS)
    c, s = turns[0, pl.ds(sht[0], 1), :COLS], turns[1, pl.ds(sht[0], 1), :COLS]
    a = jnp.concatenate([z * c, z * -s], 0)
    out = dot3(a, table[0], table[1]).reshape(2, SHT, ROWS, 2 * ORD)
    re = out[0, :, :, :ORD] + out[1, :, :, ORD:]
    im = out[1, :, :, :ORD] - out[0, :, :, ORD:]
    c, s = turns[0, :, COLS:][:, None, :], turns[1, :, COLS:][:, None, :]
    scale = 1.0 / NLON * (2.0 / (ROWS * OCEAN))
    spectra[0] = jnp.sum(re * c + im * s, axis=0) * scale
    spectra[1] = jnp.sum(im * c - re * s, axis=0) * scale
    multiply_rows(1 - core[0], y[0], spectra[...], legendre, partial)


def rows_kernel(core, y, spectra, legendre, partial):
    multiply_rows(core[0], y[0], spectra[...], legendre, partial)


def column_of(line):
    n = line.shape[1]
    row = lax.broadcasted_iota(jnp.int32, (n, n), 0)
    lane = lax.broadcasted_iota(jnp.int32, (n, n), 1)
    return jnp.sum(jnp.where(row == lane, line, 0.0), axis=1, keepdims=True)


def love_kernel(core, y, cosine_sums, one, sine_sums, two, love, loaded):
    factor = column_of(love[pl.ds(core[0] * PEERS + y[0], 1), :])
    loaded[0] = (cosine_sums[...] + one[...]) * factor
    loaded[1] = (sine_sums[...] + two[...]) * factor


def add_degrees(half, y, before, coefs, legendre):
    def some(i, acc):
        acc = list(acc)
        for k in range(PEERS):
            for n in range(2):
                tile = 2 * i + n
                degrees = degrees_of(half, y, k, tile)
                at = pl.ds(pl.multiple_of(8 * tile, 8), 8)
                x = [coefs[k][c, at, :] for c in range(2)]
                for j in range(ROWS):
                    p = legendre[j, degrees, :]
                    for c in range(2):
                        acc[c * ROWS + j] = acc[c * ROWS + j] + p * x[c]
        return tuple(acc)

    return lax.fori_loop(0, CHUNK // 16, some, tuple(before))


def degrees_kernel(core, y, *refs):
    *coefs, legendre, sums = refs
    zero = jnp.zeros((8, ORD), F32)
    acc = add_degrees(core[0], y[0], [zero] * (2 * ROWS), coefs, legendre)
    for i in range(2 * ROWS):
        sums[i] = acc[i]


def finish_kernel(core, y, before, *refs):
    *coefs, legendre, spread, synth = refs
    acc = add_degrees(1 - core[0], y[0], [before[i] for i in range(2 * ROWS)], coefs, legendre)
    for i in range(2 * ROWS):
        synth[i : i + 1, :] = jnp.sum(acc[i], axis=0, keepdims=True)
    value = synth[...]
    for t in range(SHT):
        spread[t] = value


def potential_kernel(
    core, synth, turns, doubling, high, low, level, fields, *rest
):
    *sines, pot, to_core, to_chip, sides, edges = rest
    e = doubling[...]
    s0, s1 = synth[:, 0:ROWS, :] * e, synth[:, ROWS:, :] * e
    for t in range(SHT):
        rows = slice(SHT * ROWS * t, SHT * ROWS * (t + 1))
        c, s = turns[0, t : t + 1, COLS:][None], turns[1, t : t + 1, COLS:][None]
        sides[rows, :ORD] = (s0 * c - s1 * s).reshape(SHT * ROWS, ORD)
        sides[rows, ORD:] = (s0 * s + s1 * c).reshape(SHT * ROWS, ORD)
    g = dot3(sides[...], high[...], low[...]).reshape(SHT, SHT, ROWS, 2 * COLS)
    c, s = turns[0, :, :COLS][:, None, :], turns[1, :, :COLS][:, None, :]
    for t in range(SHT):
        sal = jnp.sum(g[t, :, :, :COLS] * c - g[t, :, :, COLS:] * s, axis=0)
        value = level[t, 0:ROWS, :] - sal - fields[t, ROWS : 2 * ROWS, :]
        cols = slice(COLS * t, COLS * (t + 1))
        pot[:, cols] = value
        edges[0, 0:2, cols] = value[0:2, :]
        edges[1, 0:2, cols] = value[ROWS - 2 :, :]
        if sines:
            for side, row in ((0, 0), (1, ROWS - 1)):
                for i in range(3):
                    at = ROWS * (i + 2) + row
                    edges[side, 2 + i : 3 + i, cols] = fields[t, at : at + 1, :]
    if sines:
        wide = column_of(sines[0][...])
        for side, row in ((0, 0), (1, ROWS - 1)):
            edges[side, 5:6, :] = jnp.broadcast_to(wide[row : row + 1, :], (1, NLON))
            edges[side, 6:8, :] = jnp.zeros((2, NLON), F32)
    first_core = core[0] == 0
    to_core[...] = jnp.where(first_core, edges[1], edges[0])
    to_chip[...] = jnp.where(first_core, edges[0], edges[1])


def above_and_below(core, from_core, from_chip):
    first_core = core[0] == 0
    a, b = from_core[...], from_chip[...]
    return jnp.where(first_core, b, a), jnp.where(first_core, a, b)


def advance(field, pot, above, below, u, v, depth, damping, east_coef, coriolis):
    field[0:8, :] = jnp.zeros((8, NLON), F32)
    field[24:32, :] = jnp.zeros((8, NLON), F32)
    field[6:8, :] = above
    field[8:24, :] = pot[...]
    field[24:26, :] = below
    p = field[...]
    plus_col = lambda x: pltpu.roll(x, NLON - 1, 1)
    minus_col = lambda x: pltpu.roll(x, 1, 1)
    plus_row = lambda x: pltpu.roll(x, EROWS - 1, 0)
    minus_row = lambda x: pltpu.roll(x, 1, 0)
    ec = east_coef[...]
    old_u, old_v, f, d = u[...], v[...], coriolis[...], damping[...]
    ocean = depth[...] > 0.0
    grad_east = ec * (plus_col(p) - minus_col(p))
    grad_north = COURANT * (plus_row(p) - minus_row(p))
    new_u = jnp.where(ocean, old_u + f * old_v - grad_east - d * old_u, 0.0)
    new_v = jnp.where(ocean, old_v - f * old_u - grad_north - d * old_v, 0.0)
    flux_u, flux_v = depth[...] * new_u, depth[...] * new_v
    div = ec * (plus_col(flux_u) - minus_col(flux_u)) + COURANT * (
        plus_row(flux_v) - minus_row(flux_v)
    )
    return new_u, new_v, div, ocean


INNER = slice(8, 24)


def store_level(out, level, div, ocean):
    for t in range(SHT):
        cols = slice(COLS * t, COLS * (t + 1))
        out[t] = jnp.where(ocean[INNER, cols], level[t, 0:ROWS, :] - div[INNER, cols], 0.0)


def first_step_kernel(
    core, pot, from_core, from_chip, fields, sines,
    u, v, level, depth, damping, east_coef, coriolis, field,
):
    above, below = above_and_below(core, from_core, from_chip)
    for i, out in enumerate((u, v, depth)):
        for halo in (0, EROWS - 8):
            out[halo : halo + 8, :] = jnp.zeros((8, NLON), F32)
        out[7:8, :] = above[2 + i : 3 + i, :]
        out[24:25, :] = below[2 + i : 3 + i, :]
        for t in range(SHT):
            at = ROWS * (i + 2)
            out[INNER, COLS * t : COLS * (t + 1)] = fields[t, at : at + ROWS, :]
    coriolis[...] = jnp.zeros_like(coriolis)
    coriolis[7:8, :] = above[5:6, :]
    coriolis[INNER, :] = jnp.broadcast_to(column_of(sines[...]), (ROWS, NLON))
    coriolis[24:25, :] = below[5:6, :]
    x = coriolis[...]
    coriolis[...] = ROTATION * x
    east_coef[...] = COURANT / jnp.sqrt(1.0 - x * x)
    damping[...] = FRICTION / jnp.where(depth[...] > 0.0, depth[...], 1.0)
    new_u, new_v, div, ocean = advance(
        field, pot, above[0:2], below[0:2], u, v, depth, damping, east_coef, coriolis
    )
    u[...] = new_u
    v[...] = new_v
    store_level(level, fields, div, ocean)


def step_kernel(
    core, pot, from_core, from_chip, old_level, old_u, old_v, depth, damping, east_coef, coriolis,
    u, v, level, field,
):
    above, below = above_and_below(core, from_core, from_chip)
    new_u, new_v, div, ocean = advance(
        field, pot, above, below, old_u, old_v, depth, damping, east_coef, coriolis
    )
    u[...] = new_u
    v[...] = new_v
    store_level(level, old_level, div, ocean)


def last_step_kernel(
    sht, core, pot, from_core, from_chip, old_level, old_u, old_v, depth, damping, east_coef, coriolis,
    level, u, v, field,
):
    above, below = above_and_below(core, from_core, from_chip)
    new_u, new_v, div, _ = advance(
        field, pot, above, below, old_u, old_v, depth, damping, east_coef, coriolis
    )
    own = pl.ds(pl.multiple_of(sht[0] * COLS, COLS), COLS)
    field[...] = new_u
    u[...] = field[INNER, own]
    field[...] = new_v
    v[...] = field[INNER, own]
    field[...] = div
    level[...] = jnp.where(depth[INNER, own] > 0.0, old_level[sht[0]] - field[INNER, own], 0.0)


def shape(*dims):
    return jax.ShapeDtypeStruct(dims, F32)


PARAMS = pltpu.CompilerParams(vmem_limit_bytes=16 * 1024 * 1024)
START_PARAMS = pltpu.CompilerParams(vmem_limit_bytes=60 * 1024 * 1024)
COST = pl.CostEstimate(flops=ROWS * LDEG * ORD * 2, bytes_accessed=5 << 20, transcendentals=0)
WHOLE = pl.BlockSpec(memory_space=pltpu.VMEM)
SCALAR = pl.BlockSpec(memory_space=pltpu.SMEM)
HBM = pl.BlockSpec(memory_space=pltpu.HBM)


def whole(kernel, out_shape, scalars, *args, scratch=(), cost=None):
    return pl.pallas_call(
        kernel,
        in_specs=[SCALAR] * len(scalars) + [WHOLE] * len(args),
        out_specs=[WHOLE] * len(out_shape),
        out_shape=out_shape,
        scratch_shapes=list(scratch),
        compiler_params=PARAMS,
        cost_estimate=cost,
    )(*scalars, *args)


def per_device(height, east, north, depth, equilibrium, mask, sines, legendre, love):
    analysis, (s_high, s_low), turns, doubling = tables()
    ocean = lax.axis_index("ocean").astype(jnp.int32)
    sht = lax.axis_index("sht").astype(jnp.int32).reshape(1)
    core = (ocean & 1).reshape(1)
    y = (ocean >> 3).reshape(1)
    sines = sines.reshape(1, ROWS)
    love = love.reshape(LDEG // CHUNK, CHUNK)

    def swap(x, k):
        return lax.ppermute(x, "ocean", [(i, i ^ k) for i in range(OCEAN)])

    def swap_ring(x, k):
        pairs = []
        for i in range(OCEAN):
            for t in range(SHT):
                zeros = i % 2 == 0 and ORD * t >= LDEG // 2
                pairs.append((SHT * i + t, SHT * (i ^ (8 * k if zeros else 2 * k)) + t))
        return lax.ppermute(x, ("ocean", "sht"), pairs)

    along_y = (8, 16, 24)
    chips = [(i, (i + 1 if i % 2 else i - 1) % OCEAN) for i in range(OCEAN)]

    spread = pl.pallas_call(
        start_kernel,
        in_specs=[HBM] * 6,
        out_specs=WHOLE,
        out_shape=shape(SHT, FIELDS * ROWS, COLS),
        scratch_shapes=[
            pltpu.VMEM((FIELDS, ROWS, COLS), F32),
            pltpu.VMEM((ROWS, COLS), jnp.int32),
            pltpu.SemaphoreType.DMA((6,)),
        ],
        compiler_params=START_PARAMS,
    )(height, equilibrium, east, north, depth, mask)
    spread, sht, core, y = lax.optimization_barrier((spread, sht, core, y))
    fields = lax.all_to_all(spread, "sht", 0, 0, tiled=True)

    extended = shape(EROWS, NLON)
    block = shape(ROWS, COLS)
    partial = shape(PEERS, 2, CHUNK, ORD)
    field = [pltpu.VMEM((EROWS, NLON), F32)]
    level = fields
    for step in range(STEPS):
        given, spectra = whole(
            transform_kernel,
            [partial, shape(2, ROWS, ORD)],
            (sht, core, y),
            *(level, turns, analysis, legendre),
            cost=COST,
        )
        taken = swap(given, 1)
        (kept,) = whole(rows_kernel, [partial], (core, y), spectra, legendre, cost=COST)
        parts = [kept[k] + taken[k] for k in range(PEERS)]
        others = [swap(parts[k], along_y[k - 1]) for k in range(1, PEERS)]
        ring = (parts[0] + others[0]) + (others[1] + others[2])
        cosine_sums, sine_sums = ring[0], ring[1]
        one, two = swap_ring(cosine_sums, 1), swap_ring(sine_sums, 3)
        cosine_sums, sine_sums = cosine_sums + one, sine_sums + two
        one, two = swap_ring(cosine_sums, 3), swap_ring(sine_sums, 1)
        (coefs,) = whole(
            love_kernel,
            [shape(2, CHUNK, ORD)],
            (core, y),
            *(cosine_sums, one, sine_sums, two, love),
        )
        own_coefs = [coefs] + [swap(coefs, k) for k in along_y]
        other_coefs = [swap(x, 1) for x in own_coefs]
        (sums,) = whole(
            degrees_kernel,
            [shape(2 * ROWS, 8, ORD)],
            (core, y),
            *(*own_coefs, legendre),
            cost=COST,
        )
        (synth_spread,) = whole(
            finish_kernel,
            [shape(SHT, 2 * ROWS, ORD)],
            (core, y),
            *(sums, *other_coefs, legendre),
            scratch=[pltpu.VMEM((2 * ROWS, ORD), F32)],
            cost=COST,
        )
        synth = lax.all_to_all(synth_spread, "sht", 0, 0, tiled=True)
        halo = 8 if step == 0 else 2
        pot, to_core, to_chip = whole(
            potential_kernel,
            [shape(ROWS, NLON), shape(halo, NLON), shape(halo, NLON)],
            (core,),
            *(synth, turns, doubling, s_high, s_low, level, fields),
            *([sines] if step == 0 else []),
            scratch=[
                pltpu.VMEM((SHT * SHT * ROWS, 2 * ORD), F32),
                pltpu.VMEM((2, halo, NLON), F32),
            ],
        )
        from_chip = lax.ppermute(to_chip, "ocean", chips)
        from_core = swap(to_core, 1)
        given = (pot, from_core, from_chip)
        if step == 0:
            u, v, level, *constants = whole(
                first_step_kernel,
                [extended, extended, shape(SHT, ROWS, COLS)] + [extended] * 4,
                (core,),
                *(*given, fields, sines),
                scratch=field,
            )
        elif step < STEPS - 1:
            u, v, level = whole(
                step_kernel,
                [extended, extended, shape(SHT, ROWS, COLS)],
                (core,),
                *(*given, level, u, v, *constants),
                scratch=field,
            )
        else:
            level, u, v = whole(
                last_step_kernel,
                [block] * 3,
                (sht, core),
                *(*given, level, u, v, *constants),
                scratch=field,
            )
    return level, u, v


def solution(mesh):
    in_specs = (
        P("ocean", "sht"),
        P("ocean", "sht"),
        P("ocean", "sht"),
        P("ocean", "sht"),
        P("ocean", "sht"),
        P("ocean", "sht"),
        P("ocean"),
        P("ocean", None, "sht"),
        P(),
    )
    out_specs = (P("ocean", "sht"), P("ocean", "sht"), P("ocean", "sht"))
    return jax.shard_map(
        per_device, mesh=mesh, in_specs=in_specs, out_specs=out_specs, check_vma=False
    )
```

```python
import functools

import jax
import jax.numpy as jnp
import ml_dtypes
import numpy as np
from jax import lax
from jax.experimental import pallas as pl
from jax.experimental.pallas import tpu as pltpu
from jax.sharding import PartitionSpec as P

STEPS = 3
COURANT = 0.12
ROTATION = 0.5
FRICTION = 0.3

NLON = 2048
ROWS = 16
COLS = 256
ORD = 128
SHT = 8
OCEAN = 32
LDEG = 1024
CHUNK = 128
PEERS = 4
EROWS = 32
FIELDS = 5

F32 = jnp.float32
BF16 = jnp.bfloat16


def split(table):
    high = table.astype(ml_dtypes.bfloat16)
    low = (table - high.astype(np.float64)).astype(ml_dtypes.bfloat16)
    return high, low


def tables():
    kappa = np.arange(COLS)[:, None]
    order = np.arange(ORD)[None, :]
    turn = 2.0 * np.pi * (kappa * order % NLON) / NLON
    cosine, sine = np.cos(turn), np.sin(turn)
    analysis = np.stack(split(np.block([[cosine, sine]])))
    cosine, sine = cosine.T, sine.T
    synthesis = split(np.block([[cosine, sine], [-sine, cosine]]))

    owner = np.arange(SHT)[:, None]
    turn = 2.0 * np.pi * (np.arange(COLS)[None, :] * owner % 16) / 16
    by_owner = np.stack([np.cos(turn), np.sin(turn)], 0).astype(np.float32)
    turn = 2.0 * np.pi * (np.arange(ORD)[None, :] * owner % 8) / 8
    by_block = np.stack([np.cos(turn), np.sin(turn)], 0).astype(np.float32)
    doubling = np.full((SHT, 1, ORD), 2.0, np.float32)
    doubling[0, 0, 0] = 1.0
    turns = np.concatenate([by_owner, by_block], 2)
    return analysis, synthesis, turns, doubling


def dot3(a, high, low):
    a_high = a.astype(BF16)
    a_low = (a - a_high.astype(F32)).astype(BF16)
    dot = functools.partial(jnp.dot, preferred_element_type=F32)
    return dot(a_high, high) + (dot(a_low, high) + dot(a_high, low))


def start_kernel(height, equilibrium, east, north, depth, mask, spread, floats, ints, sems):
    copies = [
        pltpu.make_async_copy(source, floats.at[i], sems.at[i])
        for i, source in enumerate((height, equilibrium, east, north, depth))
    ]
    copies.append(pltpu.make_async_copy(mask, ints, sems.at[5]))
    for copy in copies:
        copy.start()
    for copy in copies:
        copy.wait()
    ocean = ints[...] == 1
    for i in range(FIELDS):
        field = floats[i]
        if i in (0, FIELDS - 1):
            field = jnp.where(ocean, field, 0.0)
        for t in range(SHT):
            spread[t, ROWS * i : ROWS * (i + 1), :] = field


def degrees_of(y, k, tile):
    return pl.ds(pl.multiple_of((y ^ k) * CHUNK + tile * 8, 8), 8)


def multiply_rows(y, before, weights, legendre, partial):
    wide = [
        [jnp.broadcast_to(weights[c, j : j + 1, :], (8, ORD)) for j in range(ROWS)]
        for c in range(2)
    ]

    def some(i, _):
        for k in range(PEERS):
            for n in range(2):
                tile = 2 * i + n
                degrees = degrees_of(y, k, tile)
                at = pl.ds(pl.multiple_of(8 * tile, 8), 8)
                sums = [before[k][c, at, :] if before else None for c in range(2)]
                for j in range(ROWS):
                    p = legendre[j, degrees, :]
                    for c in range(2):
                        term = p * wide[c][j]
                        sums[c] = term if sums[c] is None else sums[c] + term
                for c in range(2):
                    partial[k][c, at, :] = sums[c]
        return 0

    lax.fori_loop(0, CHUNK // 16, some, 0)


def transform_kernel(sht, level, turns, table, spectra):
    z = level[:, 0:ROWS, :].reshape(SHT * ROWS, COLS)
    c, s = turns[0, pl.ds(sht[0], 1), :COLS], turns[1, pl.ds(sht[0], 1), :COLS]
    a = jnp.concatenate([z * c, z * -s], 0)
    out = dot3(a, table[0], table[1]).reshape(2, SHT, ROWS, 2 * ORD)
    re = out[0, :, :, :ORD] + out[1, :, :, ORD:]
    im = out[1, :, :, :ORD] - out[0, :, :, ORD:]
    c, s = turns[0, :, COLS:][:, None, :], turns[1, :, COLS:][:, None, :]
    scale = 1.0 / NLON * (2.0 / (ROWS * OCEAN))
    spectra[0] = jnp.sum(re * c + im * s, axis=0) * scale
    spectra[1] = jnp.sum(im * c - re * s, axis=0) * scale


def near_rows_kernel(y, spectra, legendre, *partial):
    multiply_rows(y[0], (), spectra[...], legendre, partial)


def far_rows_kernel(y, *refs):
    before, (spectra, legendre), partial = refs[:PEERS], refs[PEERS:-PEERS], refs[-PEERS:]
    multiply_rows(y[0], before, spectra[...], legendre, partial)


def column_of(line):
    n = line.shape[1]
    row = lax.broadcasted_iota(jnp.int32, (n, n), 0)
    lane = lax.broadcasted_iota(jnp.int32, (n, n), 1)
    return jnp.sum(jnp.where(row == lane, line, 0.0), axis=1, keepdims=True)


def love_kernel(core, y, cosine_sums, one, sine_sums, two, love, loaded):
    factor = column_of(love[pl.ds(core[0] * PEERS + y[0], 1), :])
    loaded[0] = (cosine_sums[...] + one[...]) * factor
    loaded[1] = (sine_sums[...] + two[...]) * factor


def synth_kernel(y, *refs):
    *coefs, legendre, synth = refs

    def some(i, acc):
        acc = list(acc)
        for k in range(PEERS):
            for n in range(2):
                tile = 2 * i + n
                degrees = degrees_of(y[0], k, tile)
                at = pl.ds(pl.multiple_of(8 * tile, 8), 8)
                x = [coefs[k][c, at, :] for c in range(2)]
                for j in range(ROWS):
                    p = legendre[j, degrees, :]
                    for c in range(2):
                        acc[c * ROWS + j] = acc[c * ROWS + j] + p * x[c]
        return tuple(acc)

    zero = jnp.zeros((8, ORD), F32)
    acc = lax.fori_loop(0, CHUNK // 16, some, (zero,) * (2 * ROWS))
    for i in range(2 * ROWS):
        synth[i : i + 1, :] = jnp.sum(acc[i], axis=0, keepdims=True)


def potential_kernel(
    core, synth, turns, doubling, high, low, level, fields, *rest
):
    *sines, pot, to_core, to_chip, sides, edges = rest
    e = doubling[...]
    s0, s1 = synth[:, 0:ROWS, :] * e, synth[:, ROWS:, :] * e
    for t in range(SHT):
        rows = slice(SHT * ROWS * t, SHT * ROWS * (t + 1))
        c, s = turns[0, t : t + 1, COLS:][None], turns[1, t : t + 1, COLS:][None]
        sides[rows, :ORD] = (s0 * c - s1 * s).reshape(SHT * ROWS, ORD)
        sides[rows, ORD:] = (s0 * s + s1 * c).reshape(SHT * ROWS, ORD)
    g = dot3(sides[...], high[...], low[...]).reshape(SHT, SHT, ROWS, 2 * COLS)
    c, s = turns[0, :, :COLS][:, None, :], turns[1, :, :COLS][:, None, :]
    for t in range(SHT):
        sal = jnp.sum(g[t, :, :, :COLS] * c - g[t, :, :, COLS:] * s, axis=0)
        value = level[t, 0:ROWS, :] - sal - fields[t, ROWS : 2 * ROWS, :]
        cols = slice(COLS * t, COLS * (t + 1))
        pot[:, cols] = value
        edges[0, 0:2, cols] = value[0:2, :]
        edges[1, 0:2, cols] = value[ROWS - 2 :, :]
        if sines:
            for side, row in ((0, 0), (1, ROWS - 1)):
                for i in range(3):
                    at = ROWS * (i + 2) + row
                    edges[side, 2 + i : 3 + i, cols] = fields[t, at : at + 1, :]
    if sines:
        wide = column_of(sines[0][...])
        for side, row in ((0, 0), (1, ROWS - 1)):
            edges[side, 5:6, :] = jnp.broadcast_to(wide[row : row + 1, :], (1, NLON))
            edges[side, 6:8, :] = jnp.zeros((2, NLON), F32)
    first_core = core[0] == 0
    to_core[...] = jnp.where(first_core, edges[1], edges[0])
    to_chip[...] = jnp.where(first_core, edges[0], edges[1])


def above_and_below(core, from_core, from_chip):
    first_core = core[0] == 0
    a, b = from_core[...], from_chip[...]
    return jnp.where(first_core, b, a), jnp.where(first_core, a, b)


def advance(field, pot, above, below, u, v, depth, damping, east_coef, coriolis):
    field[0:8, :] = jnp.zeros((8, NLON), F32)
    field[24:32, :] = jnp.zeros((8, NLON), F32)
    field[6:8, :] = above
    field[8:24, :] = pot[...]
    field[24:26, :] = below
    p = field[...]
    plus_col = lambda x: pltpu.roll(x, NLON - 1, 1)
    minus_col = lambda x: pltpu.roll(x, 1, 1)
    plus_row = lambda x: pltpu.roll(x, EROWS - 1, 0)
    minus_row = lambda x: pltpu.roll(x, 1, 0)
    ec = east_coef[...]
    old_u, old_v, f, d = u[...], v[...], coriolis[...], damping[...]
    ocean = depth[...] > 0.0
    grad_east = ec * (plus_col(p) - minus_col(p))
    grad_north = COURANT * (plus_row(p) - minus_row(p))
    new_u = jnp.where(ocean, old_u + f * old_v - grad_east - d * old_u, 0.0)
    new_v = jnp.where(ocean, old_v - f * old_u - grad_north - d * old_v, 0.0)
    flux_u, flux_v = depth[...] * new_u, depth[...] * new_v
    div = ec * (plus_col(flux_u) - minus_col(flux_u)) + COURANT * (
        plus_row(flux_v) - minus_row(flux_v)
    )
    return new_u, new_v, div, ocean


INNER = slice(8, 24)


def store_level(out, level, div, ocean):
    for t in range(SHT):
        cols = slice(COLS * t, COLS * (t + 1))
        out[t] = jnp.where(ocean[INNER, cols], level[t, 0:ROWS, :] - div[INNER, cols], 0.0)


def first_step_kernel(
    core, pot, from_core, from_chip, fields, sines,
    u, v, level, depth, damping, east_coef, coriolis, field,
):
    above, below = above_and_below(core, from_core, from_chip)
    for i, out in enumerate((u, v, depth)):
        for halo in (0, EROWS - 8):
            out[halo : halo + 8, :] = jnp.zeros((8, NLON), F32)
        out[7:8, :] = above[2 + i : 3 + i, :]
        out[24:25, :] = below[2 + i : 3 + i, :]
        for t in range(SHT):
            at = ROWS * (i + 2)
            out[INNER, COLS * t : COLS * (t + 1)] = fields[t, at : at + ROWS, :]
    coriolis[...] = jnp.zeros_like(coriolis)
    coriolis[7:8, :] = above[5:6, :]
    coriolis[INNER, :] = jnp.broadcast_to(column_of(sines[...]), (ROWS, NLON))
    coriolis[24:25, :] = below[5:6, :]
    x = coriolis[...]
    coriolis[...] = ROTATION * x
    east_coef[...] = COURANT / jnp.sqrt(1.0 - x * x)
    damping[...] = FRICTION / jnp.where(depth[...] > 0.0, depth[...], 1.0)
    new_u, new_v, div, ocean = advance(
        field, pot, above[0:2], below[0:2], u, v, depth, damping, east_coef, coriolis
    )
    u[...] = new_u
    v[...] = new_v
    store_level(level, fields, div, ocean)


def step_kernel(
    core, pot, from_core, from_chip, old_level, old_u, old_v, depth, damping, east_coef, coriolis,
    u, v, level, field,
):
    above, below = above_and_below(core, from_core, from_chip)
    new_u, new_v, div, ocean = advance(
        field, pot, above, below, old_u, old_v, depth, damping, east_coef, coriolis
    )
    u[...] = new_u
    v[...] = new_v
    store_level(level, old_level, div, ocean)


def last_step_kernel(
    sht, core, pot, from_core, from_chip, old_level, old_u, old_v, depth, damping, east_coef, coriolis,
    level, u, v, field,
):
    above, below = above_and_below(core, from_core, from_chip)
    new_u, new_v, div, _ = advance(
        field, pot, above, below, old_u, old_v, depth, damping, east_coef, coriolis
    )
    own = pl.ds(pl.multiple_of(sht[0] * COLS, COLS), COLS)
    field[...] = new_u
    u[...] = field[INNER, own]
    field[...] = new_v
    v[...] = field[INNER, own]
    field[...] = div
    level[...] = jnp.where(depth[INNER, own] > 0.0, old_level[sht[0]] - field[INNER, own], 0.0)


def shape(*dims):
    return jax.ShapeDtypeStruct(dims, F32)


PARAMS = pltpu.CompilerParams(vmem_limit_bytes=16 * 1024 * 1024)
START_PARAMS = pltpu.CompilerParams(vmem_limit_bytes=60 * 1024 * 1024)
COST = pl.CostEstimate(flops=ROWS * LDEG * ORD * 2, bytes_accessed=5 << 20, transcendentals=0)
WHOLE = pl.BlockSpec(memory_space=pltpu.VMEM)
SCALAR = pl.BlockSpec(memory_space=pltpu.SMEM)
HBM = pl.BlockSpec(memory_space=pltpu.HBM)


def whole(kernel, out_shape, scalars, *args, scratch=(), cost=None):
    return pl.pallas_call(
        kernel,
        in_specs=[SCALAR] * len(scalars) + [WHOLE] * len(args),
        out_specs=[WHOLE] * len(out_shape),
        out_shape=out_shape,
        scratch_shapes=list(scratch),
        compiler_params=PARAMS,
        cost_estimate=cost,
    )(*scalars, *args)


def per_device(height, east, north, depth, equilibrium, mask, sines, legendre, love):
    analysis, (s_high, s_low), turns, doubling = tables()
    ocean = lax.axis_index("ocean").astype(jnp.int32)
    sht = lax.axis_index("sht").astype(jnp.int32).reshape(1)
    core = (ocean & 1).reshape(1)
    y = (ocean >> 3).reshape(1)
    sines = sines.reshape(1, ROWS)
    love = love.reshape(LDEG // CHUNK, CHUNK)

    def swap(x, k):
        return lax.ppermute(x, "ocean", [(i, i ^ k) for i in range(OCEAN)])

    def swap_ring(x, k):
        pairs = []
        for i in range(OCEAN):
            for t in range(SHT):
                zeros = i % 2 == 0 and ORD * t >= LDEG // 2
                pairs.append((SHT * i + t, SHT * (i ^ (8 * k if zeros else 2 * k)) + t))
        return lax.ppermute(x, ("ocean", "sht"), pairs)

    along_y = (8, 16, 24)
    chips = [(i, (i + 1 if i % 2 else i - 1) % OCEAN) for i in range(OCEAN)]

    spread = pl.pallas_call(
        start_kernel,
        in_specs=[HBM] * 6,
        out_specs=WHOLE,
        out_shape=shape(SHT, FIELDS * ROWS, COLS),
        scratch_shapes=[
            pltpu.VMEM((FIELDS, ROWS, COLS), F32),
            pltpu.VMEM((ROWS, COLS), jnp.int32),
            pltpu.SemaphoreType.DMA((6,)),
        ],
        compiler_params=START_PARAMS,
    )(height, equilibrium, east, north, depth, mask)
    spread, legendre = lax.optimization_barrier((spread, legendre))
    half = LDEG // 2
    near = lax.dynamic_slice_in_dim(legendre, core[0] * half, half, 1)
    far = lax.dynamic_slice_in_dim(legendre, (1 - core[0]) * half, half, 1)
    spread, near, far, sht, core, y = lax.optimization_barrier((spread, near, far, sht, core, y))
    far = swap(far, 1)
    fields = lax.all_to_all(spread, "sht", 0, 0, tiled=True)

    extended = shape(EROWS, NLON)
    block = shape(ROWS, COLS)
    chunk = shape(2, CHUNK, ORD)
    field = [pltpu.VMEM((EROWS, NLON), F32)]
    level = fields
    for step in range(STEPS):
        (spectra,) = whole(
            transform_kernel, [shape(2, ROWS, ORD)], (sht,), level, turns, analysis
        )
        far_spectra = swap(spectra, 1)
        parts = whole(near_rows_kernel, [chunk] * PEERS, (y,), spectra, near, cost=COST)
        parts = whole(
            far_rows_kernel, [chunk] * PEERS, (y,), *parts, far_spectra, far, cost=COST
        )
        others = [swap(parts[k], along_y[k - 1]) for k in range(PEERS - 1, 0, -1)]
        ring = (parts[0] + others[0]) + (others[1] + others[2])
        cosine_sums, sine_sums = ring[0], ring[1]
        one, two = swap_ring(cosine_sums, 1), swap_ring(sine_sums, 3)
        cosine_sums, sine_sums = cosine_sums + one, sine_sums + two
        one, two = swap_ring(cosine_sums, 3), swap_ring(sine_sums, 1)
        (coefs,) = whole(
            love_kernel,
            [chunk],
            (core, y),
            *(cosine_sums, one, sine_sums, two, love),
        )
        own_coefs = [coefs] + [swap(coefs, k) for k in along_y]
        rows = [shape(2 * ROWS, ORD)]
        (far_synth,) = whole(synth_kernel, rows, (y,), *own_coefs, far, cost=COST)
        returned = swap(far_synth, 1)
        (near_synth,) = whole(synth_kernel, rows, (y,), *own_coefs, near, cost=COST)
        synth_spread = jnp.broadcast_to(near_synth + returned, (SHT, 2 * ROWS, ORD))
        synth = lax.all_to_all(synth_spread, "sht", 0, 0, tiled=True)
        halo = 8 if step == 0 else 2
        pot, to_core, to_chip = whole(
            potential_kernel,
            [shape(ROWS, NLON), shape(halo, NLON), shape(halo, NLON)],
            (core,),
            *(synth, turns, doubling, s_high, s_low, level, fields),
            *([sines] if step == 0 else []),
            scratch=[
                pltpu.VMEM((SHT * SHT * ROWS, 2 * ORD), F32),
                pltpu.VMEM((2, halo, NLON), F32),
            ],
        )
        from_chip = lax.ppermute(to_chip, "ocean", chips)
        from_core = swap(to_core, 1)
        given = (pot, from_core, from_chip)
        if step == 0:
            u, v, level, *constants = whole(
                first_step_kernel,
                [extended, extended, shape(SHT, ROWS, COLS)] + [extended] * 4,
                (core,),
                *(*given, fields, sines),
                scratch=field,
            )
        elif step < STEPS - 1:
            u, v, level = whole(
                step_kernel,
                [extended, extended, shape(SHT, ROWS, COLS)],
                (core,),
                *(*given, level, u, v, *constants),
                scratch=field,
            )
        else:
            level, u, v = whole(
                last_step_kernel,
                [block] * 3,
                (sht, core),
                *(*given, level, u, v, *constants),
                scratch=field,
            )
    return level, u, v


def solution(mesh):
    in_specs = (
        P("ocean", "sht"),
        P("ocean", "sht"),
        P("ocean", "sht"),
        P("ocean", "sht"),
        P("ocean", "sht"),
        P("ocean", "sht"),
        P("ocean"),
        P("ocean", None, "sht"),
        P(),
    )
    out_specs = (P("ocean", "sht"), P("ocean", "sht"), P("ocean", "sht"))
    return jax.shard_map(
        per_device, mesh=mesh, in_specs=in_specs, out_specs=out_specs, check_vma=False
    )
```

```python
import functools

import jax
import jax.numpy as jnp
import ml_dtypes
import numpy as np
from jax import lax
from jax.experimental import pallas as pl
from jax.experimental.pallas import tpu as pltpu
from jax.sharding import PartitionSpec as P

STEPS = 3
COURANT = 0.12
ROTATION = 0.5
FRICTION = 0.3

NLON = 2048
ROWS = 16
COLS = 256
ORD = 128
SHT = 8
OCEAN = 32
LDEG = 1024
CHUNK = 128
PEERS = 4
EROWS = 32
FIELDS = 5

F32 = jnp.float32
BF16 = jnp.bfloat16


def split(table):
    high = table.astype(ml_dtypes.bfloat16)
    low = (table - high.astype(np.float64)).astype(ml_dtypes.bfloat16)
    return high, low


def tables():
    kappa = np.arange(COLS)[:, None]
    order = np.arange(ORD)[None, :]
    turn = 2.0 * np.pi * (kappa * order % NLON) / NLON
    cosine, sine = np.cos(turn), np.sin(turn)
    analysis = np.stack(split(np.block([[cosine, sine]])))
    cosine, sine = cosine.T, sine.T
    synthesis = split(np.block([[cosine, sine], [-sine, cosine]]))

    owner = np.arange(SHT)[:, None]
    turn = 2.0 * np.pi * (np.arange(COLS)[None, :] * owner % 16) / 16
    by_owner = np.stack([np.cos(turn), np.sin(turn)], 0).astype(np.float32)
    turn = 2.0 * np.pi * (np.arange(ORD)[None, :] * owner % 8) / 8
    by_block = np.stack([np.cos(turn), np.sin(turn)], 0).astype(np.float32)
    doubling = np.full((SHT, 1, ORD), 2.0, np.float32)
    doubling[0, 0, 0] = 1.0
    turns = np.concatenate([by_owner, by_block], 2)
    return analysis, synthesis, turns, doubling


def dot3(a, high, low):
    a_high = a.astype(BF16)
    a_low = (a - a_high.astype(F32)).astype(BF16)
    dot = functools.partial(jnp.dot, preferred_element_type=F32)
    return dot(a_high, high) + (dot(a_low, high) + dot(a_high, low))


def start_kernel(height, equilibrium, east, north, depth, mask, spread, floats, ints, sems):
    copies = [
        pltpu.make_async_copy(source, floats.at[i], sems.at[i])
        for i, source in enumerate((height, equilibrium, east, north, depth))
    ]
    copies.append(pltpu.make_async_copy(mask, ints, sems.at[5]))
    for copy in copies:
        copy.start()
    for copy in copies:
        copy.wait()
    ocean = ints[...] == 1
    for i in range(FIELDS):
        field = floats[i]
        if i in (0, FIELDS - 1):
            field = jnp.where(ocean, field, 0.0)
        for t in range(SHT):
            spread[t, ROWS * i : ROWS * (i + 1), :] = field


def halves_kernel(core, legendre, near, far, sems):
    half = LDEG // 2
    copies = [
        pltpu.make_async_copy(
            legendre.at[:, pl.ds(pl.multiple_of(first * half, half), half), :], out, sems.at[i]
        )
        for i, (first, out) in enumerate(((1 - core[0], far), (core[0], near)))
    ]
    for copy in copies:
        copy.start()
    for copy in copies:
        copy.wait()


def degrees_of(y, k, tile):
    return pl.ds(pl.multiple_of((y ^ k) * CHUNK + tile * 8, 8), 8)


def multiply_rows(y, before, weights, legendre, partial):
    wide = [
        [jnp.broadcast_to(weights[c, j : j + 1, :], (8, ORD)) for j in range(ROWS)]
        for c in range(2)
    ]

    def some(i, _):
        for k in range(PEERS):
            for n in range(2):
                tile = 2 * i + n
                degrees = degrees_of(y, k, tile)
                at = pl.ds(pl.multiple_of(8 * tile, 8), 8)
                sums = [before[k][c, at, :] if before else None for c in range(2)]
                for j in range(ROWS):
                    p = legendre[j, degrees, :]
                    for c in range(2):
                        term = p * wide[c][j]
                        sums[c] = term if sums[c] is None else sums[c] + term
                for c in range(2):
                    partial[k][c, at, :] = sums[c]
        return 0

    lax.fori_loop(0, CHUNK // 16, some, 0)


def transform_kernel(sht, level, turns, table, spectra):
    z = level[:, 0:ROWS, :].reshape(SHT * ROWS, COLS)
    c, s = turns[0, pl.ds(sht[0], 1), :COLS], turns[1, pl.ds(sht[0], 1), :COLS]
    a = jnp.concatenate([z * c, z * -s], 0)
    out = dot3(a, table[0], table[1]).reshape(2, SHT, ROWS, 2 * ORD)
    re = out[0, :, :, :ORD] + out[1, :, :, ORD:]
    im = out[1, :, :, :ORD] - out[0, :, :, ORD:]
    c, s = turns[0, :, COLS:][:, None, :], turns[1, :, COLS:][:, None, :]
    scale = 1.0 / NLON * (2.0 / (ROWS * OCEAN))
    spectra[0] = jnp.sum(re * c + im * s, axis=0) * scale
    spectra[1] = jnp.sum(im * c - re * s, axis=0) * scale


def near_rows_kernel(y, spectra, legendre, *partial):
    multiply_rows(y[0], (), spectra[...], legendre, partial)


def far_rows_kernel(y, *refs):
    before, (spectra, legendre), partial = refs[:PEERS], refs[PEERS:-PEERS], refs[-PEERS:]
    multiply_rows(y[0], before, spectra[...], legendre, partial)


def column_of(line):
    n = line.shape[1]
    row = lax.broadcasted_iota(jnp.int32, (n, n), 0)
    lane = lax.broadcasted_iota(jnp.int32, (n, n), 1)
    return jnp.sum(jnp.where(row == lane, line, 0.0), axis=1, keepdims=True)


def love_kernel(core, y, cosine_sums, one, sine_sums, two, love, loaded):
    factor = column_of(love[pl.ds(core[0] * PEERS + y[0], 1), :])
    loaded[0] = (cosine_sums[...] + one[...]) * factor
    loaded[1] = (sine_sums[...] + two[...]) * factor


def synth_kernel(y, *refs):
    *coefs, legendre, synth = refs

    def some(i, acc):
        acc = list(acc)
        for k in range(PEERS):
            for n in range(2):
                tile = 2 * i + n
                degrees = degrees_of(y[0], k, tile)
                at = pl.ds(pl.multiple_of(8 * tile, 8), 8)
                x = [coefs[k][c, at, :] for c in range(2)]
                for j in range(ROWS):
                    p = legendre[j, degrees, :]
                    for c in range(2):
                        acc[c * ROWS + j] = acc[c * ROWS + j] + p * x[c]
        return tuple(acc)

    zero = jnp.zeros((8, ORD), F32)
    acc = lax.fori_loop(0, CHUNK // 16, some, (zero,) * (2 * ROWS))
    for i in range(2 * ROWS):
        synth[i : i + 1, :] = jnp.sum(acc[i], axis=0, keepdims=True)


def potential_kernel(
    core, synth, turns, doubling, high, low, level, fields, *rest
):
    *sines, pot, to_core, to_chip, sides, edges = rest
    e = doubling[...]
    s0, s1 = synth[:, 0:ROWS, :] * e, synth[:, ROWS:, :] * e
    for t in range(SHT):
        rows = slice(SHT * ROWS * t, SHT * ROWS * (t + 1))
        c, s = turns[0, t : t + 1, COLS:][None], turns[1, t : t + 1, COLS:][None]
        sides[rows, :ORD] = (s0 * c - s1 * s).reshape(SHT * ROWS, ORD)
        sides[rows, ORD:] = (s0 * s + s1 * c).reshape(SHT * ROWS, ORD)
    g = dot3(sides[...], high[...], low[...]).reshape(SHT, SHT, ROWS, 2 * COLS)
    c, s = turns[0, :, :COLS][:, None, :], turns[1, :, :COLS][:, None, :]
    for t in range(SHT):
        sal = jnp.sum(g[t, :, :, :COLS] * c - g[t, :, :, COLS:] * s, axis=0)
        value = level[t, 0:ROWS, :] - sal - fields[t, ROWS : 2 * ROWS, :]
        cols = slice(COLS * t, COLS * (t + 1))
        pot[:, cols] = value
        edges[0, 0:2, cols] = value[0:2, :]
        edges[1, 0:2, cols] = value[ROWS - 2 :, :]
        if sines:
            for side, row in ((0, 0), (1, ROWS - 1)):
                for i in range(3):
                    at = ROWS * (i + 2) + row
                    edges[side, 2 + i : 3 + i, cols] = fields[t, at : at + 1, :]
    if sines:
        wide = column_of(sines[0][...])
        for side, row in ((0, 0), (1, ROWS - 1)):
            edges[side, 5:6, :] = jnp.broadcast_to(wide[row : row + 1, :], (1, NLON))
            edges[side, 6:8, :] = jnp.zeros((2, NLON), F32)
    first_core = core[0] == 0
    to_core[...] = jnp.where(first_core, edges[1], edges[0])
    to_chip[...] = jnp.where(first_core, edges[0], edges[1])


def above_and_below(core, from_core, from_chip):
    first_core = core[0] == 0
    a, b = from_core[...], from_chip[...]
    return jnp.where(first_core, b, a), jnp.where(first_core, a, b)


def advance(field, pot, above, below, u, v, depth, damping, east_coef, coriolis):
    field[0:8, :] = jnp.zeros((8, NLON), F32)
    field[24:32, :] = jnp.zeros((8, NLON), F32)
    field[6:8, :] = above
    field[8:24, :] = pot[...]
    field[24:26, :] = below
    p = field[...]
    plus_col = lambda x: pltpu.roll(x, NLON - 1, 1)
    minus_col = lambda x: pltpu.roll(x, 1, 1)
    plus_row = lambda x: pltpu.roll(x, EROWS - 1, 0)
    minus_row = lambda x: pltpu.roll(x, 1, 0)
    ec = east_coef[...]
    old_u, old_v, f, d = u[...], v[...], coriolis[...], damping[...]
    ocean = depth[...] > 0.0
    grad_east = ec * (plus_col(p) - minus_col(p))
    grad_north = COURANT * (plus_row(p) - minus_row(p))
    new_u = jnp.where(ocean, old_u + f * old_v - grad_east - d * old_u, 0.0)
    new_v = jnp.where(ocean, old_v - f * old_u - grad_north - d * old_v, 0.0)
    flux_u, flux_v = depth[...] * new_u, depth[...] * new_v
    div = ec * (plus_col(flux_u) - minus_col(flux_u)) + COURANT * (
        plus_row(flux_v) - minus_row(flux_v)
    )
    return new_u, new_v, div, ocean


INNER = slice(8, 24)


def store_level(out, level, div, ocean):
    for t in range(SHT):
        cols = slice(COLS * t, COLS * (t + 1))
        out[t] = jnp.where(ocean[INNER, cols], level[t, 0:ROWS, :] - div[INNER, cols], 0.0)


def first_step_kernel(
    core, pot, from_core, from_chip, fields, sines,
    u, v, level, depth, damping, east_coef, coriolis, field,
):
    above, below = above_and_below(core, from_core, from_chip)
    for i, out in enumerate((u, v, depth)):
        for halo in (0, EROWS - 8):
            out[halo : halo + 8, :] = jnp.zeros((8, NLON), F32)
        out[7:8, :] = above[2 + i : 3 + i, :]
        out[24:25, :] = below[2 + i : 3 + i, :]
        for t in range(SHT):
            at = ROWS * (i + 2)
            out[INNER, COLS * t : COLS * (t + 1)] = fields[t, at : at + ROWS, :]
    coriolis[...] = jnp.zeros_like(coriolis)
    coriolis[7:8, :] = above[5:6, :]
    coriolis[INNER, :] = jnp.broadcast_to(column_of(sines[...]), (ROWS, NLON))
    coriolis[24:25, :] = below[5:6, :]
    x = coriolis[...]
    coriolis[...] = ROTATION * x
    east_coef[...] = COURANT / jnp.sqrt(1.0 - x * x)
    damping[...] = FRICTION / jnp.where(depth[...] > 0.0, depth[...], 1.0)
    new_u, new_v, div, ocean = advance(
        field, pot, above[0:2], below[0:2], u, v, depth, damping, east_coef, coriolis
    )
    u[...] = new_u
    v[...] = new_v
    store_level(level, fields, div, ocean)


def step_kernel(
    core, pot, from_core, from_chip, old_level, old_u, old_v, depth, damping, east_coef, coriolis,
    u, v, level, field,
):
    above, below = above_and_below(core, from_core, from_chip)
    new_u, new_v, div, ocean = advance(
        field, pot, above, below, old_u, old_v, depth, damping, east_coef, coriolis
    )
    u[...] = new_u
    v[...] = new_v
    store_level(level, old_level, div, ocean)


def last_step_kernel(
    sht, core, pot, from_core, from_chip, old_level, old_u, old_v, depth, damping, east_coef, coriolis,
    level, u, v, field,
):
    above, below = above_and_below(core, from_core, from_chip)
    new_u, new_v, div, _ = advance(
        field, pot, above, below, old_u, old_v, depth, damping, east_coef, coriolis
    )
    own = pl.ds(pl.multiple_of(sht[0] * COLS, COLS), COLS)
    field[...] = new_u
    u[...] = field[INNER, own]
    field[...] = new_v
    v[...] = field[INNER, own]
    field[...] = div
    level[...] = jnp.where(depth[INNER, own] > 0.0, old_level[sht[0]] - field[INNER, own], 0.0)


def shape(*dims):
    return jax.ShapeDtypeStruct(dims, F32)


PARAMS = pltpu.CompilerParams(vmem_limit_bytes=16 * 1024 * 1024)
START_PARAMS = pltpu.CompilerParams(vmem_limit_bytes=60 * 1024 * 1024)
HALVES_PARAMS = pltpu.CompilerParams(vmem_limit_bytes=48 * 1024 * 1024)
COST = pl.CostEstimate(flops=ROWS * LDEG * ORD * 2, bytes_accessed=5 << 20, transcendentals=0)
WHOLE = pl.BlockSpec(memory_space=pltpu.VMEM)
SCALAR = pl.BlockSpec(memory_space=pltpu.SMEM)
HBM = pl.BlockSpec(memory_space=pltpu.HBM)


def whole(kernel, out_shape, scalars, *args, scratch=(), cost=None):
    return pl.pallas_call(
        kernel,
        in_specs=[SCALAR] * len(scalars) + [WHOLE] * len(args),
        out_specs=[WHOLE] * len(out_shape),
        out_shape=out_shape,
        scratch_shapes=list(scratch),
        compiler_params=PARAMS,
        cost_estimate=cost,
    )(*scalars, *args)


def per_device(height, east, north, depth, equilibrium, mask, sines, legendre, love):
    analysis, (s_high, s_low), turns, doubling = tables()
    ocean = lax.axis_index("ocean").astype(jnp.int32)
    sht = lax.axis_index("sht").astype(jnp.int32).reshape(1)
    core = (ocean & 1).reshape(1)
    y = (ocean >> 3).reshape(1)
    sines = sines.reshape(1, ROWS)
    love = love.reshape(LDEG // CHUNK, CHUNK)

    def swap(x, k):
        return lax.ppermute(x, "ocean", [(i, i ^ k) for i in range(OCEAN)])

    def swap_ring(x, k):
        pairs = []
        for i in range(OCEAN):
            for t in range(SHT):
                zeros = i % 2 == 0 and ORD * t >= LDEG // 2
                pairs.append((SHT * i + t, SHT * (i ^ (8 * k if zeros else 2 * k)) + t))
        return lax.ppermute(x, ("ocean", "sht"), pairs)

    along_y = (8, 16, 24)
    chips = [(i, (i + 1 if i % 2 else i - 1) % OCEAN) for i in range(OCEAN)]

    spread = pl.pallas_call(
        start_kernel,
        in_specs=[HBM] * 6,
        out_specs=WHOLE,
        out_shape=shape(SHT, FIELDS * ROWS, COLS),
        scratch_shapes=[
            pltpu.VMEM((FIELDS, ROWS, COLS), F32),
            pltpu.VMEM((ROWS, COLS), jnp.int32),
            pltpu.SemaphoreType.DMA((6,)),
        ],
        compiler_params=START_PARAMS,
    )(height, equilibrium, east, north, depth, mask)
    spread, legendre = lax.optimization_barrier((spread, legendre))
    near, far = pl.pallas_call(
        halves_kernel,
        in_specs=[SCALAR, HBM],
        out_specs=[WHOLE] * 2,
        out_shape=[shape(ROWS, LDEG // 2, ORD)] * 2,
        scratch_shapes=[pltpu.SemaphoreType.DMA((2,))],
        compiler_params=HALVES_PARAMS,
    )(core, legendre)
    spread, near, far, sht, core, y = lax.optimization_barrier((spread, near, far, sht, core, y))
    far = swap(far, 1)
    fields = lax.all_to_all(spread, "sht", 0, 0, tiled=True)

    extended = shape(EROWS, NLON)
    block = shape(ROWS, COLS)
    chunk = shape(2, CHUNK, ORD)
    field = [pltpu.VMEM((EROWS, NLON), F32)]
    level = fields
    for step in range(STEPS):
        (spectra,) = whole(
            transform_kernel, [shape(2, ROWS, ORD)], (sht,), level, turns, analysis
        )
        far_spectra = swap(spectra, 1)
        parts = whole(near_rows_kernel, [chunk] * PEERS, (y,), spectra, near, cost=COST)
        parts = whole(
            far_rows_kernel, [chunk] * PEERS, (y,), *parts, far_spectra, far, cost=COST
        )
        others = [swap(parts[k], along_y[k - 1]) for k in (2, 1, 3)]
        ring = (parts[0] + others[0]) + (others[1] + others[2])
        cosine_sums, sine_sums = ring[0], ring[1]
        one, two = swap_ring(cosine_sums, 1), swap_ring(sine_sums, 3)
        cosine_sums, sine_sums = cosine_sums + one, sine_sums + two
        one, two = swap_ring(cosine_sums, 3), swap_ring(sine_sums, 1)
        (coefs,) = whole(
            love_kernel,
            [chunk],
            (core, y),
            *(cosine_sums, one, sine_sums, two, love),
        )
        from_y = {k: swap(coefs, along_y[k - 1]) for k in (3, 1, 2)}
        own_coefs = [coefs] + [from_y[k] for k in range(1, PEERS)]
        rows = [shape(2 * ROWS, ORD)]
        (far_synth,) = whole(synth_kernel, rows, (y,), *own_coefs, far, cost=COST)
        returned = swap(far_synth, 1)
        (near_synth,) = whole(synth_kernel, rows, (y,), *own_coefs, near, cost=COST)
        synth_spread = jnp.broadcast_to(near_synth + returned, (SHT, 2 * ROWS, ORD))
        synth = lax.all_to_all(synth_spread, "sht", 0, 0, tiled=True)
        halo = 8 if step == 0 else 2
        pot, to_core, to_chip = whole(
            potential_kernel,
            [shape(ROWS, NLON), shape(halo, NLON), shape(halo, NLON)],
            (core,),
            *(synth, turns, doubling, s_high, s_low, level, fields),
            *([sines] if step == 0 else []),
            scratch=[
                pltpu.VMEM((SHT * SHT * ROWS, 2 * ORD), F32),
                pltpu.VMEM((2, halo, NLON), F32),
            ],
        )
        from_chip = lax.ppermute(to_chip, "ocean", chips)
        from_core = swap(to_core, 1)
        given = (pot, from_core, from_chip)
        if step == 0:
            u, v, level, *constants = whole(
                first_step_kernel,
                [extended, extended, shape(SHT, ROWS, COLS)] + [extended] * 4,
                (core,),
                *(*given, fields, sines),
                scratch=field,
            )
        elif step < STEPS - 1:
            u, v, level = whole(
                step_kernel,
                [extended, extended, shape(SHT, ROWS, COLS)],
                (core,),
                *(*given, level, u, v, *constants),
                scratch=field,
            )
        else:
            level, u, v = whole(
                last_step_kernel,
                [block] * 3,
                (sht, core),
                *(*given, level, u, v, *constants),
                scratch=field,
            )
    return level, u, v


def solution(mesh):
    in_specs = (
        P("ocean", "sht"),
        P("ocean", "sht"),
        P("ocean", "sht"),
        P("ocean", "sht"),
        P("ocean", "sht"),
        P("ocean", "sht"),
        P("ocean"),
        P("ocean", None, "sht"),
        P(),
    )
    out_specs = (P("ocean", "sht"), P("ocean", "sht"), P("ocean", "sht"))
    return jax.shard_map(
        per_device, mesh=mesh, in_specs=in_specs, out_specs=out_specs, check_vma=False
    )
```
